32 devices in a mesh: seg: 8 (over z, y), col: 4 (over x, core).
Axes of the slice: x: 2, y: 2, z: 4, core: 2. Of those that a mesh axis runs over, the one named last changes fastest.
Arguments:
- model_mixing: float32 [16, 384, 384], P('seg', 'col'), may hold values from -0.07654656 to 0.07654656
- retention: float32 [16, 384], P('seg'), may hold values from 0.5 to 0.95
- forcing: float32 [16, 384], P('seg'), may hold values from -1.2 to 1.2
- observations: float32 [16, 1024], P('seg'), may hold values from -6 to 6
- model_noise: float32 [16, 384], P('seg'), may hold values from 0.01 to 0.1
- obs_noise: float32 [1024], replicated, may hold values from 0.5 to 2
- gain: float32 [384, 1024], replicated, may hold values from -0.01875 to 0.01875
- obs_operator_t: float32 [384, 1024], P('col'), may hold values from -0.30618623 to 0.30618623
- prior_mean: float32 [384], replicated, may hold values from -6 to 6
- prior_factor: float32 [384, 384], replicated, may hold values from -0.3125 to 0.3125
Outputs:
- means: float32 [16, 384], P('seg')
- covariances: float32 [16, 384, 384], P('seg', 'col')
The draws below stay inside these ranges and needn't reach their ends.
All inputs are finite; a program needn't handle non-finite values.
Results may differ from the reference program's by a relative error of at most 0.00019.
Values sent between devices are 32-bit elements; how exact they have to be, the bound alone decides.
No kernel may reach another device: no remote copies, remote signals or barrier semaphores. Data moves between devices by JAX's collectives and lax.ppermute only.
A program may use at most 64 MiB of HBM per device.

```python
import math
import jax
import jax.numpy as jnp
from jax import lax

N = 384
NOBS = 1024
WINDOW = 16


def shard_levels(stream_key, shape, split, low, largest):
    level = 1.0
    for axis_at, shards_of in split:
        heights = jax.random.uniform(jax.random.fold_in(jax.random.fold_in(stream_key, 6), axis_at), (shards_of,), jnp.float32, low / len(split), largest / len(split))
        level = level * jnp.repeat(jnp.exp(heights), shape[axis_at] // shards_of).reshape((-1,) + (1,) * (len(shape) - 1 - axis_at))
    return level


def bell_draw(stream_key, extent, spread, most, shards=(), held_as=jnp.bfloat16):
    drawn = spread * jax.random.normal(stream_key, extent, jnp.float32)
    if shards:
        drawn = drawn * shard_levels(stream_key, extent, shards, -0.22, 0.18)
    return jnp.clip(drawn, -most, most).astype(held_as)


def setup_inputs(seed: int = 0) -> dict:
    key_list = jax.random.split(jax.random.key(seed), 11)
    return {
        "model_mixing": bell_draw(key_list[0], (WINDOW, N, N), (0.25 / N ** 0.5), 0.07654656, ((0, 8), (1, 4)), jnp.float32),
        "retention": jnp.clip(jnp.exp(math.log(0.95) - 0.64185387 * jax.random.uniform(key_list[1], (WINDOW, N), jnp.float32) ** shard_levels(key_list[1], (WINDOW, N), ((0, 8),), -0.2, 0.2)), 0.5, 0.95),
        "forcing": bell_draw(key_list[2], (WINDOW, N), 0.2, 1.2, ((0, 8),), jnp.float32),
        "observations": bell_draw(key_list[3], (WINDOW, NOBS), 1.0, 6.0, ((0, 8),), jnp.float32),
        "model_noise": jnp.clip(jnp.exp(math.log(0.1) - 2.3025851 * jax.random.uniform(key_list[4], (WINDOW, N), jnp.float32) ** shard_levels(key_list[4], (WINDOW, N), ((0, 8),), -0.2, 0.2)), 0.01, 0.1),
        "obs_noise": jnp.clip(jnp.exp(jax.random.uniform(key_list[5], (NOBS,), jnp.float32, math.log(0.5), math.log(2.0))), 0.5, 2.0),
        "gain": bell_draw(key_list[6], (N, NOBS), (0.1 / NOBS ** 0.5), 0.01875, (), jnp.float32),
        "obs_operator_t": bell_draw(key_list[7], (N, NOBS), (1.0 / N ** 0.5), 0.30618623, ((0, 4),), jnp.float32),
        "prior_mean": bell_draw(key_list[8], (N,), 1.0, 6.0, (), jnp.float32),
        "prior_factor": bell_draw(key_list[9], (N, N), N ** -0.5, 0.3125, (), jnp.float32),
    }


precise = lax.Precision.HIGHEST


def product(left, right):
    return jnp.dot(left, right, precision=precise, preferred_element_type=jnp.float32)


def reference(model_mixing, retention, forcing, observations, model_noise, obs_noise, gain, obs_operator_t, prior_mean, prior_factor):
    identity = jnp.eye(N, dtype=jnp.float32)
    correction = identity - product(gain, obs_operator_t.T)
    fixed_noise = product(gain * obs_noise[None, :], gain.T)

    def advance(carried, inputs):
        mean_now, covar_now = carried
        mixing, keeping, pushing, observed, variances = inputs
        model_step = jnp.diag(keeping) + mixing.T
        step_matrix = product(correction, model_step)
        step_offset = product(correction, pushing) + product(gain, observed)
        step_noise = product(correction * variances[None, :], correction.T) + fixed_noise
        mean_next = product(step_matrix, mean_now) + step_offset
        covar_next = product(product(step_matrix, covar_now), step_matrix.T) + step_noise
        return (mean_next, covar_next), (mean_next, covar_next)

    initial = (prior_mean, product(prior_factor, prior_factor.T))
    final_pair, outputs = lax.scan(advance, initial, (model_mixing, retention, forcing, observations, model_noise))
    return outputs[0], outputs[1]
```

```python
import jax
import jax.numpy as jnp
from jax import lax
from jax.sharding import PartitionSpec as P

three_pass = lax.Precision.HIGH


def dot_nn(left, right):
    return lax.dot_general(
        left,
        right,
        (((1,), (0,)), ((), ())),
        precision=three_pass,
        preferred_element_type=jnp.float32,
    )


def dot_nt(left, right):
    return lax.dot_general(
        left,
        right,
        (((1,), (1,)), ((), ())),
        precision=three_pass,
        preferred_element_type=jnp.float32,
    )


def sandwich(step, covar):
    return dot_nt(dot_nn(step, covar), step)


def swapped(block, axis, bit):
    return lax.ppermute(block, axis, [(i, i ^ bit) for i in range(lax.axis_size(axis))])


def shifted(block, axis, distance):
    size = lax.axis_size(axis)
    return lax.ppermute(block, axis, [(i, i + distance) for i in range(size - distance)])


def in_order(blocks, offsets, me):
    stacked = jnp.stack(blocks)
    inverse = {offset: at for at, offset in enumerate(offsets)}
    table = jnp.array([inverse[offset] for offset in range(len(offsets))])
    ordered = [
        lax.dynamic_index_in_dim(stacked, table[device ^ me], 0, keepdims=False)
        for device in range(len(offsets))
    ]
    return jnp.concatenate(ordered, axis=-2)


def per_device(
    model_mixing,
    retention,
    forcing,
    observations,
    model_noise,
    obs_noise,
    gain,
    obs_operator_t,
    prior_mean,
    prior_factor,
):
    steps, width, states = model_mixing.shape
    n_col, n_seg = lax.axis_size("col"), lax.axis_size("seg")
    col, seg = lax.axis_index("col"), lax.axis_index("seg")
    core = col % 2
    far_bits = []
    bit = n_col // 2
    while bit > 1:
        far_bits.append(bit)
        bit //= 2

    own = [model_mixing]
    for bit in far_bits:
        own = own + [swapped(b, "col", bit) for b in own]
    offsets = [0]
    for bit in far_bits:
        offsets = offsets + [o ^ bit for o in offsets]
    near = swapped(model_mixing, "seg", 1)
    vectors = jnp.concatenate([retention, model_noise, forcing, observations], axis=1)
    vectors_other = swapped(vectors, "seg", 1)

    row_ids = lax.broadcasted_iota(jnp.int32, (width, states), 0) + col * width
    col_ids = lax.broadcasted_iota(jnp.int32, (width, states), 1)
    corr_rows = (row_ids == col_ids).astype(jnp.float32) - dot_nt(obs_operator_t, gain)
    corr = [corr_rows]
    for bit in far_bits:
        corr = corr + [swapped(b, "col", bit) for b in corr]

    other_first = [near[:1]] + [swapped(b[:1], "seg", 1) for b in own[1:]]
    other_rest = [near[1:]]
    for bit in far_bits:
        other_rest = other_rest + [swapped(b, "col", bit) for b in other_rest]
    other = [jnp.concatenate(pair, axis=0) for pair in zip(other_first, other_rest)]

    def over_core(blocks):
        both = swapped(jnp.stack(blocks), "col", 1)
        return blocks + [both[i] for i in range(len(blocks))]

    offsets_all = offsets + [o ^ 1 for o in offsets]
    own_full = in_order(over_core(own), offsets_all, col)
    corr_t = in_order(over_core(corr), offsets_all, col)
    other_full = in_order(over_core(other), offsets_all, col)

    correction = corr_t.T
    fixed_noise = dot_nt(gain * obs_noise[None, :], gain)
    prior_covar = dot_nt(prior_factor, prior_factor)

    is_second = seg % 2 == 1
    is_first_group = seg < 2
    mixing_first = jnp.where(is_second, other_full, own_full)
    mixing_second = jnp.where(is_second, own_full, other_full)
    vectors_first = jnp.where(is_second, vectors_other, vectors)
    vectors_second = jnp.where(is_second, vectors, vectors_other)
    mixing = jnp.concatenate([mixing_first, mixing_second], axis=0)
    packed = jnp.concatenate([vectors_first, vectors_second], axis=0)
    keep, noise_var, push, seen = jnp.split(packed, [states, 2 * states, 3 * states], axis=1)
    eye = jnp.eye(states, dtype=jnp.float32)
    offset_each = dot_nt(push, correction) + dot_nt(seen, gain)

    total_covar = jnp.where(is_first_group, prior_covar, 0.0)
    total_mean = jnp.where(is_first_group, prior_mean, 0.0)[None, :]
    total_step = None
    marks = []
    for k in range(2 * steps):
        step = dot_nt(correction, mixing[k] + keep[k][:, None] * eye)
        noise = dot_nt(correction * noise_var[k][None, :], correction) + fixed_noise
        total_covar = sandwich(step, total_covar) + noise
        total_mean = dot_nt(total_mean, step) + offset_each[k][None, :]
        total_step = step if total_step is None else dot_nn(step, total_step)
        marks.append((total_step, total_mean, total_covar))

    half = states // 2
    pad = jnp.zeros((7, states), jnp.float32)

    def carried_along(matrix, vector, distance):
        part = lax.dynamic_slice_in_dim(matrix, core * half, half, 0)
        if vector is not None:
            part = jnp.concatenate([part, vector, pad], axis=0)
        came = shifted(part, "seg", distance)
        swap = swapped(came[:half], "col", 1)
        low = jnp.where(core == 0, came[:half], swap)
        high = jnp.where(core == 0, swap, came[:half])
        full = jnp.concatenate([low, high], axis=0)
        return full, (came[half : half + 1] if vector is not None else None)

    entry_covar, entry_mean = carried_along(total_covar, total_mean, 2)
    distance = 4
    entry_step = None
    if distance < n_seg:
        entry_step, ignored = carried_along(total_step, None, 2)
    while distance < n_seg:
        sent_covar = sandwich(total_step, entry_covar) + total_covar
        sent_mean = dot_nt(entry_mean, total_step) + total_mean
        came_covar, came_mean = carried_along(sent_covar, sent_mean, distance)
        if 2 * distance < n_seg:
            sent_step = dot_nn(total_step, entry_step)
            came_step, ignored = carried_along(sent_step, None, distance)
        entry_covar = sandwich(entry_step, came_covar) + entry_covar
        entry_mean = dot_nt(came_mean, entry_step) + entry_mean
        if 2 * distance < n_seg:
            entry_step = dot_nn(entry_step, came_step)
        distance *= 2

    means, covars = [], []
    for k in range(steps):
        step = jnp.where(is_second, marks[steps + k][0], marks[k][0])
        mean = jnp.where(is_second, marks[steps + k][1], marks[k][1])
        covar = jnp.where(is_second, marks[steps + k][2], marks[k][2])
        rows = lax.dynamic_slice_in_dim(step, col * width, width, 0)
        covar_rows = lax.dynamic_slice_in_dim(covar, col * width, width, 0)
        means.append(dot_nt(entry_mean, step) + mean)
        covars.append(dot_nt(dot_nn(rows, entry_covar), step) + covar_rows)
    return jnp.concatenate(means, axis=0), jnp.stack(covars)


def solution(mesh):
    in_specs = (
        P("seg", "col", None),
        P("seg", None),
        P("seg", None),
        P("seg", None),
        P("seg", None),
        P(),
        P(),
        P("col", None),
        P(),
        P(),
    )
    out_specs = (P("seg", None), P("seg", "col", None))
    return jax.shard_map(
        per_device, mesh=mesh, in_specs=in_specs, out_specs=out_specs, check_vma=False
    )
```

```python
import functools

import jax
import jax.numpy as jnp
from jax import lax
from jax.experimental import pallas as pl
from jax.experimental.pallas import tpu as pltpu
from jax.sharding import PartitionSpec as P

F32, BF16 = jnp.float32, jnp.bfloat16
NN = (((1,), (0,)), ((), ()))
NT = (((1,), (1,)), ((), ()))
MEAN_ROWS = 16


def parts(x):
    high = x.astype(BF16)
    return high, (x - high.astype(F32)).astype(BF16)


def as_left(x):
    high, low = parts(x)
    return jnp.concatenate([high, high, low], axis=1)


def as_right(x, axis):
    high, low = parts(x)
    return jnp.concatenate([high, low, high], axis=axis)


def dot_nn(left, right):
    return lax.dot_general(as_left(left), as_right(right, 0), NN, preferred_element_type=F32)


def dot_nt(left, right):
    return lax.dot_general(as_left(left), as_right(right, 1), NT, preferred_element_type=F32)


def square(step, covar, mean):
    rows = covar.shape[0]
    both = dot_nt(jnp.concatenate([dot_nn(step, covar), mean], axis=0), step)
    return both[:rows], both[rows:]


def mean_block(row, states):
    return jnp.broadcast_to(row, (MEAN_ROWS, states))


def local_call(body, outs, *operands, scratch=(), products=1.0):
    states = outs[0][-1]
    shapes = [jax.ShapeDtypeStruct(shape, F32) for shape in outs]
    return pl.pallas_call(
        body,
        out_shape=shapes,
        scratch_shapes=[pltpu.VMEM(shape, F32) for shape in scratch],
        compiler_params=pltpu.CompilerParams(vmem_limit_bytes=36 * 2**20),
        cost_estimate=pl.CostEstimate(
            flops=int(products * 6 * 384**3), bytes_accessed=4 * states, transcendentals=0
        ),
    )(*operands)


def correction_rows(oper_ref, gain_ref, out_ref):
    width, states = out_ref.shape
    rows = lax.broadcasted_iota(jnp.int32, (width, states), 0) + lax.axis_index("col") * width
    cols = lax.broadcasted_iota(jnp.int32, (width, states), 1)
    out_ref[...] = (rows == cols).astype(F32) - dot_nt(oper_ref[...], gain_ref[...])


def fixed_parts(gain_ref, noise_ref, factor_ref, seen_ref, fixed_ref, prior_ref, pushed_ref):
    states = gain_ref.shape[0]
    gain = gain_ref[...]
    both = dot_nt(jnp.concatenate([gain * noise_ref[...], seen_ref[...]], axis=0), gain)
    fixed_ref[...] = both[:states]
    pushed_ref[...] = both[states:]
    first = (lax.axis_index("seg") < 2).astype(F32)
    prior_ref[...] = dot_nt(factor_ref[...], factor_ref[...]) * first


def place(pieces, offsets, out_ref, base):
    me = lax.axis_index("col")
    width = pieces[0].shape[-2]
    for piece, offset in zip(pieces, offsets):
        at = pl.multiple_of((me ^ offset) * width + base, 8)
        out_ref[pl.ds(at, width), :] = piece


def noises(offsets, vec_ref, pushed_ref, fixed_ref, *refs):
    pieces, (corr_ref, noise_ref, offset_ref, work_ref) = refs[:-4], refs[-4:]
    states = corr_ref.shape[0]
    every = vec_ref.shape[0]
    place([p[...] for p in pieces], offsets, work_ref, 0)
    corr = work_ref[...].T
    corr_ref[...] = corr
    right = as_right(corr, 1)
    push = jnp.concatenate(
        [vec_ref[:, 2 * states : 3 * states]] + [jnp.zeros((MEAN_ROWS - every, states), F32)], axis=0
    )
    left = [corr * vec_ref[k : k + 1, states : 2 * states] for k in range(every)] + [push]
    for k in range(every):
        noise = lax.dot_general(as_left(left[k]), right, NT, preferred_element_type=F32)
        noise_ref[k] = noise + fixed_ref[...]
    pushed = lax.dot_general(as_left(push), right, NT, preferred_element_type=F32) + pushed_ref[...]
    for k in range(every):
        offset_ref[k] = mean_block(pushed[k : k + 1], states)


def step_matrices(pieces, offsets, corr, keep_ref, base, work_ref):
    states = corr.shape[0]
    for k, of_step in enumerate(pieces):
        place(of_step, offsets, work_ref, k * states)
    mixed = dot_nt(corr, work_ref[...])
    return [
        mixed[:, k * states : (k + 1) * states] + corr * keep_ref[base + k : base + k + 1, :states]
        for k in range(len(pieces))
    ]


def own_segment(offsets, steps, vec_ref, corr_ref, noise_ref, offset_ref, prior_ref, start_ref, *refs):
    pieces, (psi_ref, covar_ref, mean_ref, work_ref) = refs[:-4], refs[-4:]
    states = corr_ref.shape[0]
    of_steps = [[p[k] for p in pieces] for k in range(steps)]
    matrices = step_matrices(of_steps, offsets, corr_ref[...], vec_ref, 0, work_ref)
    covar_ref[0] = noise_ref[0]
    mean_ref[0] = offset_ref[0]

    @pl.when(lax.axis_index("seg") == 0)
    def _():
        start = mean_block(start_ref[...], states)
        covar, mean = square(matrices[0], prior_ref[...], start)
        covar_ref[0] += covar
        mean_ref[0] += mean

    psi_ref[0] = matrices[0]
    for k in range(1, steps):
        covar, mean = square(matrices[k], covar_ref[k - 1], mean_ref[k - 1])
        covar_ref[k] = covar + noise_ref[k]
        mean_ref[k] = mean + offset_ref[k]
        psi_ref[k] = dot_nn(matrices[k], psi_ref[k - 1])


def put_packed(step_ref, covar, mean, blocks, out_ref):
    states = covar.shape[0]
    edge = states // 3
    core = lax.rem(lax.axis_index("col"), 2)

    @pl.when(core == 0)
    def _():
        rows = step_ref[: 2 * edge, :]
        low = dot_nt(dot_nn(rows, covar), rows)
        out_ref[:edge, :] = low[:edge, :edge] + blocks(0, 0)
        out_ref[edge : 2 * edge, :] = low[edge:, :edge] + blocks(1, 0)
        out_ref[2 * edge : 3 * edge, :] = low[edge:, edge:] + blocks(1, 1)
        out_ref[3 * edge :, :] = jnp.zeros((8, edge), F32)

    @pl.when(core == 1)
    def _():
        rows = step_ref[2 * edge :, :]
        both = dot_nt(jnp.concatenate([dot_nn(rows, covar), mean], axis=0), step_ref[...])
        out_ref[3 * edge :, :] = jnp.zeros((8, edge), F32)
        for j in range(3):
            at = slice(j * edge, (j + 1) * edge)
            out_ref[at, :] = both[:edge, at] + blocks(2, j)
            out_ref[3 * edge + j : 3 * edge + j + 1, :] = both[edge : edge + 1, at] + blocks(3, j)


def unpacked(mine_ref, mate_ref, covar_ref):
    states = covar_ref.shape[0]
    edge = states // 3
    is_low = lax.rem(lax.axis_index("col"), 2) == 0
    low = jnp.where(is_low, mine_ref[...], mate_ref[...])
    high = jnp.where(is_low, mate_ref[...], mine_ref[...])

    def put(i, j, block):
        covar_ref[i * edge : (i + 1) * edge, j * edge : (j + 1) * edge] = block
        if i != j:
            covar_ref[j * edge : (j + 1) * edge, i * edge : (i + 1) * edge] = block.T

    put(0, 0, low[:edge])
    put(1, 0, low[edge : 2 * edge])
    put(1, 1, low[2 * edge : 3 * edge])
    for j in range(3):
        put(2, j, high[j * edge : (j + 1) * edge])
    row = jnp.concatenate([high[3 * edge + j : 3 * edge + j + 1] for j in range(3)], axis=1)
    return mean_block(row, states)


def other_segment(
    offsets, steps, vec_ref, corr_ref, noise_ref, offset_ref, prior_ref, start_ref, psi_ref, covar_ref, mean_ref, *refs
):
    n_piece = len(offsets)
    firsts, rests = refs[:n_piece], refs[n_piece : 2 * n_piece]
    matrix_ref, psi_other_ref, covar_other_ref, mean_other_ref, out_ref, work_ref, after_ref = refs[2 * n_piece :]
    states = corr_ref.shape[0]
    is_second = lax.rem(lax.axis_index("seg"), 2) == 1
    of_steps = [[p[0] for p in firsts]] + [[p[k] for p in rests] for k in range(steps - 1)]
    matrices = step_matrices(of_steps, offsets, corr_ref[...], vec_ref, steps, work_ref)
    for k in range(steps):
        matrix_ref[k] = matrices[k]
    covar_other_ref[...] = noise_ref[steps]
    mean_other_ref[...] = offset_ref[steps]

    @pl.when(lax.axis_index("seg") == 1)
    def _():
        start = mean_block(start_ref[...], states)
        covar, mean = square(matrices[0], prior_ref[...], start)
        covar_other_ref[...] += covar
        mean_other_ref[...] += mean

    for k in range(1, steps):
        covar, mean = square(matrices[k], covar_other_ref[...], mean_other_ref[...])
        covar_other_ref[...] = covar + noise_ref[steps + k]
        mean_other_ref[...] = mean + offset_ref[steps + k]

    @pl.when(is_second)
    def _():
        after_ref[...] = psi_ref[steps - 1]

    @pl.when(jnp.logical_not(is_second))
    def _():
        psi_other_ref[...] = matrices[0]
        for k in range(1, steps):
            psi_other_ref[...] = dot_nn(matrices[k], psi_other_ref[...])
        after_ref[...] = psi_other_ref[...]

    edge = states // 3
    own_covar, own_mean = covar_ref[steps - 1], mean_ref[steps - 1]
    covar = jnp.where(is_second, covar_other_ref[...], own_covar)
    mean = jnp.where(is_second, mean_other_ref[...], own_mean)

    def blocks(i, j):
        at = slice(j * edge, (j + 1) * edge)
        if i == 3:
            return jnp.where(is_second, own_mean[:1, at], mean_other_ref[:1, at])
        rows = slice(i * edge, (i + 1) * edge)
        return jnp.where(is_second, covar_ref[steps - 1, rows, at], covar_other_ref[rows, at])

    put_packed(after_ref, covar, mean, blocks, out_ref)


def pair_elements(steps, width, psi_ref, covar_ref, mean_ref, matrix_ref, psi_other_ref, covar_other_ref, mean_other_ref, *refs):
    psi_out_ref, covar_out_ref, mean_out_ref, psi_all_ref, send_ref = refs
    states = psi_all_ref.shape[0]
    is_second = lax.rem(lax.axis_index("seg"), 2) == 1
    mine = pl.ds(pl.multiple_of(lax.axis_index("col") * width, 8), width)

    @pl.when(is_second)
    def _():
        before = matrix_ref[0]
        for k in range(1, steps):
            before = dot_nn(matrix_ref[k], before)
        covar, mean = covar_other_ref[...], mean_other_ref[...]
        for k in range(steps):
            psi_out_ref[k] = dot_nn(psi_ref[k], before)
            half = dot_nn(psi_ref[k, mine, :], covar)
            both = dot_nt(jnp.concatenate([half, mean], axis=0), psi_ref[k])
            covar_out_ref[k] = both[:width] + covar_ref[k, mine, :]
            mean_out_ref[k] = both[width:] + mean_ref[k]
        psi_all_ref[...] = psi_out_ref[steps - 1]

    @pl.when(jnp.logical_not(is_second))
    def _():
        for k in range(steps):
            psi_out_ref[k] = psi_ref[k]
            covar_out_ref[k] = covar_ref[k, mine, :]
            mean_out_ref[k] = mean_ref[k]
        psi_all_ref[...] = dot_nn(psi_other_ref[...], psi_ref[steps - 1])

    half = states // 2
    core = lax.rem(lax.axis_index("col"), 2)
    send_ref[...] = psi_all_ref[pl.ds(pl.multiple_of(core * half, 8), half), :]


def packed_blocks(ref, edge):
    def blocks(i, j):
        if i == 3:
            return ref[3 * edge + j : 3 * edge + j + 1, :]
        at = (i + j) if i < 2 else j
        return ref[at * edge : (at + 1) * edge, :]

    return blocks


def carried_on(step_ref, added_ref, mine_ref, mate_ref, out_ref, work_ref):
    mean = unpacked(mine_ref, mate_ref, work_ref)
    put_packed(step_ref, work_ref[...], mean, packed_blocks(added_ref, out_ref.shape[1]), out_ref)


def whole_matrix(mine_ref, mate_ref):
    is_low = lax.rem(lax.axis_index("col"), 2) == 0
    mine, mate = mine_ref[...], mate_ref[...]
    return jnp.concatenate([jnp.where(is_low, mine, mate), jnp.where(is_low, mate, mine)], axis=0)


def matrix_on(step_mine_ref, mine_ref, mate_ref, out_ref):
    out_ref[...] = dot_nn(step_mine_ref[...], whole_matrix(mine_ref, mate_ref))


def joined(mine_ref, mate_ref, out_ref):
    out_ref[...] = whole_matrix(mine_ref, mate_ref)


def entered(steps, width, psi_ref, covar_ref, mean_ref, mine_ref, mate_ref, step_mine_ref, step_mate_ref, *refs):
    psi_out_ref, covar_out_ref, mean_out_ref, work_ref = refs
    mine = pl.ds(pl.multiple_of(lax.axis_index("col") * width, 8), width)
    before = whole_matrix(step_mine_ref, step_mate_ref)
    mean = unpacked(mine_ref, mate_ref, work_ref)
    covar = work_ref[...]
    for k in range(steps):
        psi_out_ref[k] = dot_nn(psi_ref[k], before)
        half = dot_nn(psi_ref[k, mine, :], covar)
        both = dot_nt(jnp.concatenate([half, mean], axis=0), psi_ref[k])
        covar_out_ref[k] = both[:width] + covar_ref[k]
        mean_out_ref[k] = both[width:] + mean_ref[k]


def finished(steps, width, psi_ref, covar_ref, mean_ref, mine_ref, mate_ref, covar_out_ref, mean_out_ref, work_ref):
    mine = pl.ds(pl.multiple_of(lax.axis_index("col") * width, 8), width)
    mean = unpacked(mine_ref, mate_ref, work_ref)
    rows = jnp.concatenate([psi_ref[k, mine, :] for k in range(steps)], axis=0)
    half = dot_nn(rows, work_ref[...])
    for k in range(steps):
        part = half[k * width : (k + 1) * width]
        both = dot_nt(jnp.concatenate([part, mean], axis=0), psi_ref[k])
        covar_out_ref[k] = both[:width] + covar_ref[k]
        mean_out_ref[k : k + 1, :] = both[width : width + 1] + mean_ref[k, :1, :]


def swapped(block, axis, bit):
    return lax.ppermute(block, axis, [(i, i ^ bit) for i in range(lax.axis_size(axis))])


def shifted(block, distance):
    size = lax.axis_size("seg")
    return lax.ppermute(block, "seg", [(i, i + distance) for i in range(size - distance)])


def per_device(
    model_mixing,
    retention,
    forcing,
    observations,
    model_noise,
    obs_noise,
    gain,
    obs_operator_t,
    prior_mean,
    prior_factor,
):
    steps, width, states = model_mixing.shape
    n_col, n_seg = lax.axis_size("col"), lax.axis_size("seg")
    edge = states // 3
    far_bits = []
    bit = n_col // 2
    while bit > 1:
        far_bits.append(bit)
        bit //= 2
    offsets = [0]
    for bit in far_bits:
        offsets = offsets + [o ^ bit for o in offsets]
    offsets = offsets + [o ^ 1 for o in offsets]

    own = [model_mixing]
    for bit in far_bits:
        own = own + [swapped(b, "col", bit) for b in own]
    near = swapped(model_mixing, "seg", 1)
    vectors = jnp.concatenate([retention, model_noise, forcing, observations], axis=1)
    vectors_other = swapped(vectors, "seg", 1)

    (corr_mine,) = local_call(
        correction_rows, [(width, states)], obs_operator_t, gain, products=0.7
    )
    corr = [corr_mine]
    for bit in far_bits:
        corr = corr + [swapped(b, "col", bit) for b in corr]

    other_first = [near[:1]] + [swapped(b[:1], "seg", 1) for b in own[1:]]
    other_rest = [near[1:]]
    for bit in far_bits:
        other_rest = other_rest + [swapped(b, "col", bit) for b in other_rest]

    def over_core(blocks):
        return list(blocks) + [swapped(b, "col", 1) for b in blocks]

    own = over_core(own)
    corr = over_core(corr)
    other_first = over_core(other_first)
    other_rest = over_core(other_rest)

    all_vectors = jnp.concatenate([vectors, vectors_other], axis=0)
    seen = jnp.pad(all_vectors[:, 3 * states :], ((0, MEAN_ROWS - 2 * steps), (0, 0)))
    fixed, prior, pushed = local_call(
        fixed_parts,
        [(states, states), (states, states), (MEAN_ROWS, states)],
        gain,
        obs_noise[None, :],
        prior_factor,
        seen,
        products=4,
    )
    square_shape, mean_shape = (states, states), (MEAN_ROWS, states)
    correction, noise, offset = local_call(
        functools.partial(noises, offsets),
        [square_shape, (2 * steps,) + square_shape, (2 * steps,) + mean_shape],
        all_vectors,
        pushed,
        fixed,
        *corr,
        scratch=[square_shape],
        products=4,
    )
    start = prior_mean[None, :]
    psi, covar, mean = local_call(
        functools.partial(own_segment, offsets, steps),
        [(steps,) + square_shape, (steps,) + square_shape, (steps,) + mean_shape],
        all_vectors,
        correction,
        noise,
        offset,
        prior,
        start,
        *own,
        scratch=[(steps * states, states)],
        products=5,
    )
    share = (3 * edge + 8, edge)
    matrix, psi_other, covar_other, mean_other, total = local_call(
        functools.partial(other_segment, offsets, steps),
        [(steps,) + square_shape, square_shape, square_shape, mean_shape, share],
        all_vectors,
        correction,
        noise,
        offset,
        prior,
        start,
        psi,
        covar,
        mean,
        *other_first,
        *other_rest,
        scratch=[(steps * states, states), square_shape],
        products=7,
    )

    entry = shifted(total, 2)
    psi, covar, mean, psi_all, psi_half = local_call(
        functools.partial(pair_elements, steps, width),
        [(steps,) + square_shape, (steps, width, states), (steps,) + mean_shape, square_shape, (states // 2, states)],
        psi,
        covar,
        mean,
        matrix,
        psi_other,
        covar_other,
        mean_other,
        products=4,
    )
    entry = (entry, swapped(entry, "col", 1))
    distance = 4
    if distance < n_seg:
        step = shifted(psi_half, 2)
        step = (step, swapped(step, "col", 1))
    while distance < n_seg:
        more = 2 * distance < n_seg
        (sent,) = local_call(
            carried_on, [share], psi_all, total, *entry, scratch=[square_shape], products=1.5
        )
        came = shifted(sent, distance)
        if more:
            (sent,) = local_call(matrix_on, [(states // 2, states)], psi_half, *step)
            came_step = shifted(sent, distance)
            came_step = (came_step, swapped(came_step, "col", 1))
            came = (came, swapped(came, "col", 1))
            (whole,) = local_call(joined, [square_shape], *step)
            (entry_mine,) = local_call(
                carried_on, [share], whole, entry[0], *came, scratch=[square_shape], products=1.5
            )
            (step_mine,) = local_call(matrix_on, [(states // 2, states)], step[0], *came_step)
            entry = (entry_mine, swapped(entry_mine, "col", 1))
            step = (step_mine, swapped(step_mine, "col", 1))
        else:
            psi, covar, mean = local_call(
                functools.partial(entered, steps, width),
                [(steps,) + square_shape, (steps, width, states), (steps,) + mean_shape],
                psi,
                covar,
                mean,
                *entry,
                *step,
                scratch=[square_shape],
                products=4,
            )
            entry = (came, swapped(came, "col", 1))
        distance *= 2

    covars, means = local_call(
        functools.partial(finished, steps, width),
        [(steps, width, states), (steps, states)],
        psi,
        covar,
        mean,
        *entry,
        scratch=[square_shape],
        products=1.5,
    )
    return means, covars


def solution(mesh):
    in_specs = (
        P("seg", "col", None),
        P("seg", None),
        P("seg", None),
        P("seg", None),
        P("seg", None),
        P(),
        P(),
        P("col", None),
        P(),
        P(),
    )
    out_specs = (P("seg", None), P("seg", "col", None))
    return jax.shard_map(
        per_device, mesh=mesh, in_specs=in_specs, out_specs=out_specs, check_vma=False
    )
```

```python
import functools

import jax
import jax.numpy as jnp
from jax import lax
from jax.experimental import pallas as pl
from jax.experimental.pallas import tpu as pltpu
from jax.sharding import PartitionSpec as P

F32, BF16 = jnp.float32, jnp.bfloat16
NN = (((1,), (0,)), ((), ()))
NT = (((1,), (1,)), ((), ()))
MEAN_ROWS = 16
COST = 7 * 10**8


def parts(x):
    high = x.astype(BF16)
    return high, (x - high.astype(F32)).astype(BF16)


def as_left(x):
    high, low = parts(x)
    return jnp.concatenate([high, high, low], axis=1)


def as_right(x, axis):
    high, low = parts(x)
    return jnp.concatenate([high, low, high], axis=axis)


def dot_nn(left, right):
    return lax.dot_general(as_left(left), as_right(right, 0), NN, preferred_element_type=F32)


def dot_nt(left, right):
    return lax.dot_general(as_left(left), as_right(right, 1), NT, preferred_element_type=F32)


def square(step, covar, mean):
    rows = covar.shape[0]
    both = dot_nt(jnp.concatenate([dot_nn(step, covar), mean], axis=0), step)
    return both[:rows], both[rows:]


def mean_block(row, states):
    return jnp.broadcast_to(row, (MEAN_ROWS, states))


def local_call(body, outs, *operands, scratch=(), copied=False, cost=0):
    shapes = [jax.ShapeDtypeStruct(shape, F32) for shape in outs]
    return pl.pallas_call(
        body,
        out_shape=shapes,
        name=getattr(body, "func", body).__name__,
        in_specs=[pl.BlockSpec(memory_space=pltpu.HBM if copied else pltpu.VMEM)] * len(operands),
        scratch_shapes=[pltpu.VMEM(o.shape, F32) for o in operands if copied]
        + [pltpu.SemaphoreType.DMA((len(operands),))] * copied
        + [pltpu.VMEM(shape, F32) for shape in scratch],
        compiler_params=pltpu.CompilerParams(vmem_limit_bytes=(58 if copied else 36) * 2**20),
        cost_estimate=pl.CostEstimate(
            flops=cost * COST, bytes_accessed=4096, transcendentals=0
        ),
    )(*operands)


def by_gain(left, right):
    return lax.dot_general(as_left(left), right, NT, preferred_element_type=F32)


def correction_rows(
    gain_hbm, oper_hbm, seen_hbm, keep_hbm, push_hbm, var_hbm, corr_ref, vec_ref,
    gain_ref, oper_ref, seen_ref, keep_ref, push_ref, var_ref, sems,
):
    moves = [
        pltpu.make_async_copy(source, target, sems.at[i])
        for i, (source, target) in enumerate(
            [
                (gain_hbm, gain_ref),
                (oper_hbm, oper_ref),
                (seen_hbm, seen_ref),
                (keep_hbm, keep_ref),
                (push_hbm, push_ref),
                (var_hbm, var_ref),
            ]
        )
    ]
    for move in moves:
        move.start()
    width, states = corr_ref.shape
    steps = keep_ref.shape[0]
    rows = lax.broadcasted_iota(jnp.int32, (width, states), 0) + lax.axis_index("col") * width
    cols = lax.broadcasted_iota(jnp.int32, (width, states), 1)
    for move in moves:
        move.wait()
    blank = jnp.zeros((MEAN_ROWS - steps, gain_ref.shape[1]), F32)
    left = jnp.concatenate([oper_ref[...], seen_ref[...], blank], axis=0)
    both = by_gain(left, as_right(gain_ref[...], 1))
    corr_ref[...] = (rows == cols).astype(F32) - both[:width]
    for k in range(steps):
        here = slice(k, k + 1)
        vec_ref[k, 0:1, :] = keep_ref[here, :]
        vec_ref[k, 1:2, :] = var_ref[here, :]
        vec_ref[k, 2:3, :] = push_ref[here, :]
        vec_ref[k, 3:4, :] = both[width + k : width + k + 1]


def fixed_parts(gain_ref, noise_ref, factor_ref, fixed_ref, prior_ref):
    gain = gain_ref[...]
    fixed_ref[...] = by_gain(gain * noise_ref[...], as_right(gain, 1))

    @pl.when(lax.axis_index("seg") < 2)
    def _():
        prior_ref[...] = dot_nt(factor_ref[...], factor_ref[...])


def place(pieces, offsets, out_ref, base):
    me = lax.axis_index("col")
    width = pieces[0].shape[-2]
    for piece, offset in zip(pieces, offsets):
        at = pl.multiple_of((me ^ offset) * width + base, 8)
        out_ref[pl.ds(at, width), :] = piece


def noises(offsets, vec_ref, vec_other_ref, fixed_ref, *refs):
    pieces, (corr_ref, noise_ref, offset_ref, work_ref) = refs[:-4], refs[-4:]
    states = corr_ref.shape[0]
    steps = vec_ref.shape[0]
    place([p[...] for p in pieces], offsets, work_ref, 0)
    corr = work_ref[...].T
    corr_ref[...] = corr
    right = as_right(corr, 1)
    vectors = [vec_ref[k] for k in range(steps)] + [vec_other_ref[k] for k in range(steps)]
    push = [v[2:3] for v in vectors] + [jnp.zeros((MEAN_ROWS - 2 * steps, states), F32)]
    left = jnp.concatenate([corr * v[1:2] for v in vectors] + push, axis=0)
    both = lax.dot_general(as_left(left), right, NT, preferred_element_type=F32)
    base = 2 * steps * states
    for k in range(2 * steps):
        noise_ref[k] = both[k * states : (k + 1) * states] + fixed_ref[...]
        offset_ref[k] = mean_block(both[base + k : base + k + 1] + vectors[k][3:4], states)


def mixed_rows(steps_of, corr_ref, *refs):
    pieces, (out_ref,) = refs[:-1], refs[-1:]
    width = pieces[0].shape[1]
    blocks = [(k, piece[i]) for piece, of in zip(pieces, steps_of) for i, k in enumerate(of)]
    mixed = dot_nt(jnp.concatenate([block for _, block in blocks], axis=0), corr_ref[...])
    filled = [0] * out_ref.shape[0]
    for i, (k, _) in enumerate(blocks):
        out_ref[k, filled[k] : filled[k] + width, :] = mixed[i * width : (i + 1) * width]
        filled[k] += width


def matrices_of(offsets, vec_ref, corr, mine_ref, mate_ref, work_ref, out_ref):
    steps, half, states = mine_ref.shape
    width = half // len(offsets)
    for k in range(steps):
        for ref, bit in ((mine_ref, 0), (mate_ref, 1)):
            blocks = [ref[k, i * width : (i + 1) * width, :] for i in range(len(offsets))]
            place(blocks, [o ^ bit for o in offsets], work_ref, 0)
        out_ref[k] = work_ref[...].T + corr * vec_ref[k, 0:1, :]


def all_matrices(
    offsets, vec_ref, vec_other_ref, corr_ref, mine_ref, mate_ref, mine_other_ref, mate_other_ref,
    matrix_ref, psi_ref, matrix_other_ref, psi_other_ref, psi_half_ref, work_ref, work_other_ref,
):
    steps, half, states = mine_ref.shape
    seg = lax.axis_index("seg")
    is_second = lax.rem(seg, 2) == 1
    corr = corr_ref[...]
    matrices_of(offsets, vec_ref, corr, mine_ref, mate_ref, work_ref, matrix_ref)
    matrices_of(offsets, vec_other_ref, corr, mine_other_ref, mate_other_ref, work_other_ref, matrix_other_ref)
    mine = pl.ds(pl.multiple_of(lax.rem(lax.axis_index("col"), 2) * half, 8), half)
    psi_ref[0] = matrix_ref[0]
    for k in range(1, steps):
        psi_ref[k] = dot_nn(matrix_ref[k], psi_ref[k - 1])

    @pl.when(seg >= 2)
    def _():
        psi_other_ref[...] = matrix_other_ref[0]
        for k in range(1, steps):
            psi_other_ref[...] = dot_nn(matrix_other_ref[k], psi_other_ref[...])

        @pl.when(is_second)
        def _():
            psi_half_ref[...] = dot_nn(psi_ref[steps - 1, mine, :], psi_other_ref[...])

        @pl.when(jnp.logical_not(is_second))
        def _():
            psi_half_ref[...] = dot_nn(psi_other_ref[mine, :], psi_ref[steps - 1])


def put_packed(step_ref, covar, mean, blocks, out_ref):
    states = covar.shape[0]
    edge = states // 3
    core = lax.rem(lax.axis_index("col"), 2)

    @pl.when(core == 0)
    def _():
        rows = step_ref[: 2 * edge, :]
        low = dot_nt(dot_nn(rows, covar), rows)
        out_ref[:edge, :] = low[:edge, :edge] + blocks(0, 0)
        out_ref[edge : 2 * edge, :] = low[edge:, :edge] + blocks(1, 0)
        out_ref[2 * edge : 3 * edge, :] = low[edge:, edge:] + blocks(1, 1)
        out_ref[3 * edge :, :] = jnp.zeros((8, edge), F32)

    @pl.when(core == 1)
    def _():
        rows = step_ref[2 * edge :, :]
        both = dot_nt(jnp.concatenate([dot_nn(rows, covar), mean], axis=0), step_ref[...])
        out_ref[3 * edge :, :] = jnp.zeros((8, edge), F32)
        for j in range(3):
            at = slice(j * edge, (j + 1) * edge)
            out_ref[at, :] = both[:edge, at] + blocks(2, j)
            out_ref[3 * edge + j : 3 * edge + j + 1, :] = both[edge : edge + 1, at] + blocks(3, j)


def unpacked(mine_ref, mate_ref, covar_ref):
    states = covar_ref.shape[0]
    edge = states // 3
    is_low = lax.rem(lax.axis_index("col"), 2) == 0
    low = jnp.where(is_low, mine_ref[...], mate_ref[...])
    high = jnp.where(is_low, mate_ref[...], mine_ref[...])

    def put(i, j, block):
        covar_ref[i * edge : (i + 1) * edge, j * edge : (j + 1) * edge] = block
        if i != j:
            covar_ref[j * edge : (j + 1) * edge, i * edge : (i + 1) * edge] = block.T

    put(0, 0, low[:edge])
    put(1, 0, low[edge : 2 * edge])
    put(1, 1, low[2 * edge : 3 * edge])
    for j in range(3):
        put(2, j, high[j * edge : (j + 1) * edge])
    row = jnp.concatenate([high[3 * edge + j : 3 * edge + j + 1] for j in range(3)], axis=1)
    return mean_block(row, states)


def pair_covariance(
    steps, noise_ref, offset_ref, prior_ref, start_ref, matrix_ref, psi_ref, matrix_other_ref,
    covar_ref, mean_ref, covar_other_ref, mean_other_ref, out_ref, step_ref,
):
    states = prior_ref.shape[0]
    edge = states // 3
    seg = lax.axis_index("seg")
    is_second = lax.rem(seg, 2) == 1
    last = steps - 1
    covar_ref[0] = noise_ref[0]
    mean_ref[0] = offset_ref[0]

    def with_prior(step):
        return square(step, prior_ref[...], mean_block(start_ref[...], states))

    @pl.when(seg == 0)
    def _():
        covar, mean = with_prior(matrix_ref[0])
        covar_ref[0] += covar
        mean_ref[0] += mean

    for k in range(1, steps):
        covar, mean = square(matrix_ref[k], covar_ref[k - 1], mean_ref[k - 1])
        covar_ref[k] = covar + noise_ref[k]
        mean_ref[k] = mean + offset_ref[k]

    @pl.when(is_second)
    def _():
        covar_other_ref[...] = noise_ref[steps]
        mean_other_ref[...] = offset_ref[steps]
        step_ref[...] = psi_ref[last]

        @pl.when(seg == 1)
        def _():
            covar, mean = with_prior(matrix_other_ref[0])
            covar_other_ref[...] += covar
            mean_other_ref[...] += mean

    @pl.when(jnp.logical_not(is_second))
    def _():
        covar_other_ref[...] = covar_ref[last]
        mean_other_ref[...] = mean_ref[last]
        step_ref[...] = matrix_other_ref[last]

    def one_step(k):
        covar, mean = square(matrix_other_ref[k], covar_other_ref[...], mean_other_ref[...])
        covar_other_ref[...] = covar + noise_ref[steps + k]
        mean_other_ref[...] = mean + offset_ref[steps + k]

    for k in range(last):
        one_step(k + is_second.astype(jnp.int32))

    def blocks(i, j):
        at = slice(j * edge, (j + 1) * edge)
        if i == 3:
            return jnp.where(is_second, mean_ref[last, :1, at], offset_ref[steps + last, :1, at])
        rows = slice(i * edge, (i + 1) * edge)
        return jnp.where(is_second, covar_ref[last, rows, at], noise_ref[steps + last, rows, at])

    put_packed(step_ref, covar_other_ref[...], mean_other_ref[...], blocks, out_ref)


def pair_elements(steps, width, psi_ref, covar_ref, mean_ref, psi_other_ref, covar_other_ref, mean_other_ref, *refs):
    psi_out_ref, covar_out_ref, mean_out_ref, psi_all_ref = refs
    seg = lax.axis_index("seg")
    is_second = lax.rem(seg, 2) == 1
    mine = pl.ds(pl.multiple_of(lax.axis_index("col") * width, 8), width)

    @pl.when(seg < 2)
    def _():
        psi_out_ref[...] = jnp.zeros_like(psi_out_ref)

    @pl.when(seg >= 2)
    def _():
        for k in range(steps):

            @pl.when(is_second)
            def _():
                psi_out_ref[k] = dot_nn(psi_ref[k], psi_other_ref[...])

            @pl.when(jnp.logical_not(is_second))
            def _():
                psi_out_ref[k] = psi_ref[k]

        @pl.when(is_second)
        def _():
            psi_all_ref[...] = psi_out_ref[steps - 1]

        @pl.when(jnp.logical_not(is_second))
        def _():
            psi_all_ref[...] = dot_nn(psi_other_ref[...], psi_ref[steps - 1])

    @pl.when(is_second)
    def _():
        covar, mean = covar_other_ref[...], mean_other_ref[...]
        for k in range(steps):
            half = dot_nn(psi_ref[k, mine, :], covar)
            both = dot_nt(jnp.concatenate([half, mean], axis=0), psi_ref[k])
            covar_out_ref[k] = both[:width] + covar_ref[k, mine, :]
            mean_out_ref[k] = both[width:] + mean_ref[k]

    @pl.when(jnp.logical_not(is_second))
    def _():
        for k in range(steps):
            covar_out_ref[k] = covar_ref[k, mine, :]
            mean_out_ref[k] = mean_ref[k]


def packed_blocks(ref, edge):
    def blocks(i, j):
        if i == 3:
            return ref[3 * edge + j : 3 * edge + j + 1, :]
        at = (i + j) if i < 2 else j
        return ref[at * edge : (at + 1) * edge, :]

    return blocks


def carried_on(distance, step_ref, added_ref, mine_ref, mate_ref, out_ref, work_ref):
    @pl.when(lax.axis_index("seg") < lax.axis_size("seg") - distance)
    def _():
        mean = unpacked(mine_ref, mate_ref, work_ref)
        put_packed(step_ref, work_ref[...], mean, packed_blocks(added_ref, out_ref.shape[1]), out_ref)


def whole_matrix(mine_ref, mate_ref):
    is_low = lax.rem(lax.axis_index("col"), 2) == 0
    mine, mate = mine_ref[...], mate_ref[...]
    return jnp.concatenate([jnp.where(is_low, mine, mate), jnp.where(is_low, mate, mine)], axis=0)


def matrix_on(step_mine_ref, mine_ref, mate_ref, out_ref):
    out_ref[...] = dot_nn(step_mine_ref[...], whole_matrix(mine_ref, mate_ref))


def joined(mine_ref, mate_ref, out_ref):
    out_ref[...] = whole_matrix(mine_ref, mate_ref)


def entered(steps, width, psi_ref, covar_ref, mean_ref, mine_ref, mate_ref, step_mine_ref, step_mate_ref, *refs):
    psi_out_ref, covar_out_ref, mean_out_ref, work_ref = refs
    mine = pl.ds(pl.multiple_of(lax.axis_index("col") * width, 8), width)
    before = whole_matrix(step_mine_ref, step_mate_ref)
    mean = unpacked(mine_ref, mate_ref, work_ref)
    covar = work_ref[...]
    for k in range(steps):
        psi_out_ref[k] = dot_nn(psi_ref[k], before)
        half = dot_nn(psi_ref[k, mine, :], covar)
        both = dot_nt(jnp.concatenate([half, mean], axis=0), psi_ref[k])
        covar_out_ref[k] = both[:width] + covar_ref[k]
        mean_out_ref[k] = both[width:] + mean_ref[k]


def finished(steps, width, psi_ref, covar_ref, mean_ref, *refs):
    shares, (covar_out_ref, mean_out_ref, mine_ref, mate_ref, work_ref) = refs[:-5], refs[-5:]
    mine_ref[...] = sum(r[...] for r in shares[0::2])
    mate_ref[...] = sum(r[...] for r in shares[1::2])
    mine = pl.ds(pl.multiple_of(lax.axis_index("col") * width, 8), width)
    mean = unpacked(mine_ref, mate_ref, work_ref)
    rows = jnp.concatenate([psi_ref[k, mine, :] for k in range(steps)], axis=0)
    half = dot_nn(rows, work_ref[...])
    for k in range(steps):
        part = half[k * width : (k + 1) * width]
        both = dot_nt(jnp.concatenate([part, mean], axis=0), psi_ref[k])
        covar_out_ref[k] = both[:width] + covar_ref[k]
        mean_out_ref[k : k + 1, :] = both[width : width + 1] + mean_ref[k, :1, :]


def swapped(block, axis, bit):
    return lax.ppermute(block, axis, [(i, i ^ bit) for i in range(lax.axis_size(axis))])


def shifted(block, distance, start=0, stop=None):
    size = lax.axis_size("seg")
    stop = size - distance if stop is None else stop
    return lax.ppermute(block, "seg", [(i, i + distance) for i in range(start, stop)])


def with_mate(share):
    return (share, swapped(share, "col", 1))


def per_device(
    model_mixing,
    retention,
    forcing,
    observations,
    model_noise,
    obs_noise,
    gain,
    obs_operator_t,
    prior_mean,
    prior_factor,
):
    steps, width, states = model_mixing.shape
    n_col, n_seg = lax.axis_size("col"), lax.axis_size("seg")
    edge = states // 3
    square_shape, mean_shape = (states, states), (MEAN_ROWS, states)
    share_shape, half_shape = (3 * edge + 8, edge), (states // 2, states)
    far_bits = []
    bit = n_col // 2
    while bit > 1:
        far_bits.append(bit)
        bit //= 2
    offsets = [0]
    for bit in far_bits:
        offsets = offsets + [o ^ bit for o in offsets]

    own = [model_mixing]
    for bit in far_bits:
        own = own + [swapped(b, "col", bit) for b in own]
    near = swapped(model_mixing, "seg", 1)
    corr_mine, vectors = local_call(
        correction_rows,
        [(width, states), (steps, 4, states)],
        gain,
        obs_operator_t,
        observations,
        retention,
        forcing,
        model_noise,
        copied=True,
        cost=3,
    )
    corr = [corr_mine]
    for bit in far_bits:
        corr = corr + [swapped(b, "col", bit) for b in corr]
    vectors_other = swapped(vectors, "seg", 1)
    fixed, prior = local_call(
        fixed_parts, [square_shape, square_shape], gain, obs_noise[None, :], prior_factor
    )
    own, near, fixed = lax.optimization_barrier((own, near, fixed))
    other_first = [near[:1]] + [swapped(b[:1], "seg", 1) for b in own[1:]]
    other_rest = [near[1:]]
    for bit in far_bits:
        other_rest = other_rest + [swapped(b, "col", bit) for b in other_rest]
    corr, vectors_other, fixed = lax.optimization_barrier((corr, vectors_other, fixed))
    corr = corr + [swapped(b, "col", 1) for b in corr]

    correction, noise, offset = local_call(
        functools.partial(noises, offsets + [o ^ 1 for o in offsets]),
        [square_shape, (2 * steps,) + square_shape, (2 * steps,) + mean_shape],
        vectors,
        vectors_other,
        fixed,
        *corr,
        scratch=[square_shape],
    )
    rows_shape = (steps,) + half_shape
    every = list(range(steps))
    (rows,) = local_call(
        functools.partial(mixed_rows, [every] * len(own)), [rows_shape], correction, *own
    )
    other_first, other_rest, correction, noise, rows = lax.optimization_barrier(
        (other_first, other_rest, correction, noise, rows)
    )
    (rows_other,) = local_call(
        functools.partial(mixed_rows, [every[:1]] * len(own) + [every[1:]] * len(own)),
        [rows_shape],
        correction,
        *other_first,
        *other_rest,
    )
    matrix, psi, matrix_other, psi_other, psi_half = local_call(
        functools.partial(all_matrices, offsets),
        [(steps,) + square_shape, (steps,) + square_shape, (steps,) + square_shape, square_shape, half_shape],
        vectors,
        vectors_other,
        correction,
        *with_mate(rows),
        *with_mate(rows_other),
        scratch=[square_shape, square_shape],
    )
    if n_seg > 4:
        step = shifted(psi_half, 2, 2)
    covar, mean, covar_other, mean_other, total = local_call(
        functools.partial(pair_covariance, steps),
        [(steps,) + square_shape, (steps,) + mean_shape, square_shape, mean_shape, share_shape],
        noise,
        offset,
        prior,
        prior_mean[None, :],
        matrix,
        psi,
        matrix_other,
        scratch=[square_shape],
    )
    entry = shifted(total, 2)
    psi, covar, mean, psi_all = local_call(
        functools.partial(pair_elements, steps, width),
        [(steps,) + square_shape, (steps, width, states), (steps,) + mean_shape, square_shape],
        psi,
        covar,
        mean,
        psi_other,
        covar_other,
        mean_other,
    )
    if n_seg > 4:
        entry, psi_all, step = lax.optimization_barrier((entry, psi_all, step))
    entry = with_mate(entry)
    entries = [entry]
    distance = 4
    while distance < n_seg:
        more = 2 * distance < n_seg
        (sent,) = local_call(
            functools.partial(carried_on, distance), [share_shape], psi_all, total, *entry, scratch=[square_shape]
        )
        step, sent = lax.optimization_barrier((step, sent))
        step = with_mate(step)
        if more:
            came = with_mate(shifted(sent, distance))
            (sent,) = local_call(matrix_on, [half_shape], psi_half, *step)
            came_step = with_mate(shifted(sent, distance))
            (whole,) = local_call(joined, [square_shape], *step)
            (entry,) = local_call(
                functools.partial(carried_on, 0), [share_shape], whole, entry[0], *came, scratch=[square_shape]
            )
            entry = with_mate(entry)
            (step,) = local_call(matrix_on, [half_shape], step[0], *came_step)
        else:
            early = shifted(total, distance, 0, 2)
            came = shifted(sent, distance, 2)
            psi, covar, mean = local_call(
                functools.partial(entered, steps, width),
                [(steps,) + square_shape, (steps, width, states), (steps,) + mean_shape],
                psi,
                covar,
                mean,
                *entry,
                *step,
                scratch=[square_shape],
            )
            came, psi = lax.optimization_barrier((came, psi))
            entries = [with_mate(early), with_mate(came)]
        distance *= 2

    covars, means = local_call(
        functools.partial(finished, steps, width),
        [(steps, width, states), (steps, states)],
        psi,
        covar,
        mean,
        *[share for pair in entries for share in pair],
        scratch=[share_shape, share_shape, square_shape],
    )
    return means, covars


def solution(mesh):
    in_specs = (
        P("seg", "col", None),
        P("seg", None),
        P("seg", None),
        P("seg", None),
        P("seg", None),
        P(),
        P(),
        P("col", None),
        P(),
        P(),
    )
    out_specs = (P("seg", None), P("seg", "col", None))
    return jax.shard_map(
        per_device, mesh=mesh, in_specs=in_specs, out_specs=out_specs, check_vma=False
    )
```

```python
import functools

import jax
import jax.numpy as jnp
from jax import lax
from jax.experimental import pallas as pl
from jax.experimental.pallas import tpu as pltpu
from jax.sharding import PartitionSpec as P

F32, BF16 = jnp.float32, jnp.bfloat16
NN = (((1,), (0,)), ((), ()))
NT = (((1,), (1,)), ((), ()))
MEAN_ROWS = 16
COST = 7 * 10**8


def parts(x):
    high = x.astype(BF16)
    return high, (x - high.astype(F32)).astype(BF16)


def as_left(x):
    high, low = parts(x)
    return jnp.concatenate([high, high, low], axis=1)


def as_right(x, axis):
    high, low = parts(x)
    return jnp.concatenate([high, low, high], axis=axis)


def dot_nn(left, right):
    return lax.dot_general(as_left(left), as_right(right, 0), NN, preferred_element_type=F32)


def dot_nt(left, right):
    return lax.dot_general(as_left(left), as_right(right, 1), NT, preferred_element_type=F32)


def square(step, covar, mean):
    rows = covar.shape[0]
    both = dot_nt(jnp.concatenate([dot_nn(step, covar), mean], axis=0), step)
    return both[:rows], both[rows:]


def mean_block(row, states):
    return jnp.broadcast_to(row, (MEAN_ROWS, states))


def local_call(body, outs, *operands, scratch=(), copied=False, cost=0):
    shapes = [jax.ShapeDtypeStruct(shape, F32) for shape in outs]
    return pl.pallas_call(
        body,
        out_shape=shapes,
        name=getattr(body, "func", body).__name__,
        in_specs=[pl.BlockSpec(memory_space=pltpu.HBM if copied else pltpu.VMEM)] * len(operands),
        scratch_shapes=[pltpu.VMEM(o.shape, F32) for o in operands if copied]
        + [pltpu.SemaphoreType.DMA((len(operands),))] * copied
        + [pltpu.VMEM(shape, F32) for shape in scratch],
        compiler_params=pltpu.CompilerParams(vmem_limit_bytes=(58 if copied else 36) * 2**20),
        cost_estimate=pl.CostEstimate(
            flops=cost * COST, bytes_accessed=4096, transcendentals=0
        ),
    )(*operands)


def by_gain(left, right):
    return lax.dot_general(as_left(left), right, NT, preferred_element_type=F32)


def correction_rows(
    gain_hbm, oper_hbm, seen_hbm, keep_hbm, push_hbm, var_hbm, corr_ref, vec_ref,
    gain_ref, oper_ref, seen_ref, keep_ref, push_ref, var_ref, sems,
):
    moves = [
        pltpu.make_async_copy(source, target, sems.at[i])
        for i, (source, target) in enumerate(
            [
                (gain_hbm, gain_ref),
                (oper_hbm, oper_ref),
                (seen_hbm, seen_ref),
                (keep_hbm, keep_ref),
                (push_hbm, push_ref),
                (var_hbm, var_ref),
            ]
        )
    ]
    for move in moves:
        move.start()
    width, states = corr_ref.shape
    steps = keep_ref.shape[0]
    rows = lax.broadcasted_iota(jnp.int32, (width, states), 0) + lax.axis_index("col") * width
    cols = lax.broadcasted_iota(jnp.int32, (width, states), 1)
    for move in moves:
        move.wait()
    blank = jnp.zeros((MEAN_ROWS - steps, gain_ref.shape[1]), F32)
    left = jnp.concatenate([oper_ref[...], seen_ref[...], blank], axis=0)
    both = by_gain(left, as_right(gain_ref[...], 1))
    corr_ref[...] = (rows == cols).astype(F32) - both[:width]
    for k in range(steps):
        here = slice(k, k + 1)
        vec_ref[k, 0:1, :] = keep_ref[here, :]
        vec_ref[k, 1:2, :] = var_ref[here, :]
        vec_ref[k, 2:3, :] = push_ref[here, :]
        vec_ref[k, 3:4, :] = both[width + k : width + k + 1]


def fixed_parts(gain_ref, noise_ref, factor_ref, fixed_ref, prior_ref):
    gain = gain_ref[...]
    fixed_ref[...] = by_gain(gain * noise_ref[...], as_right(gain, 1))

    @pl.when(lax.axis_index("seg") < 2)
    def _():
        prior_ref[...] = dot_nt(factor_ref[...], factor_ref[...])


def place(pieces, offsets, out_ref, base):
    me = lax.axis_index("col")
    width = pieces[0].shape[-2]
    for piece, offset in zip(pieces, offsets):
        at = pl.multiple_of((me ^ offset) * width + base, 8)
        out_ref[pl.ds(at, width), :] = piece


def noises(vec_ref, vec_other_ref, fixed_ref, corr_ref, noise_ref, offset_ref):
    states = corr_ref.shape[0]
    steps = vec_ref.shape[0]
    corr = corr_ref[...]
    vectors = [vec_ref[k] for k in range(steps)] + [vec_other_ref[k] for k in range(steps)]
    push = [v[2:3] for v in vectors] + [jnp.zeros((MEAN_ROWS - 2 * steps, states), F32)]
    left = jnp.concatenate([corr * v[1:2] for v in vectors] + push, axis=0)
    both = dot_nt(left, corr)
    base = 2 * steps * states
    for k in range(2 * steps):
        noise_ref[k] = both[k * states : (k + 1) * states] + fixed_ref[...]
        offset_ref[k] = mean_block(both[base + k : base + k + 1] + vectors[k][3:4], states)


def mixed_rows(out_ref, pieces, corr):
    steps, width = pieces[0].shape[:2]
    rows = jnp.concatenate([piece[k] for k in range(steps) for piece in pieces], axis=0)
    mixed = dot_nt(rows, corr)
    half = width * len(pieces)
    for k in range(steps):
        out_ref[k] = mixed[k * half : (k + 1) * half]


def own_rows(offsets, *refs):
    n_piece = len(offsets)
    pieces, own, (corr_ref, out_ref, work_ref) = refs[:n_piece], refs[n_piece:-3], refs[-3:]
    place([p[...] for p in pieces], offsets, work_ref, 0)
    corr_ref[...] = work_ref[...].T
    mixed_rows(out_ref, own, corr_ref[...])


def other_rows(corr_ref, *refs):
    mixed_rows(refs[-1], refs[:-1], corr_ref[...])


def matrices_of(offsets, vec_ref, corr, mine_ref, mate_ref, work_ref, out_ref):
    steps, half, states = mine_ref.shape
    width = half // len(offsets)
    for k in range(steps):
        for ref, bit in ((mine_ref, 0), (mate_ref, 1)):
            blocks = [ref[k, i * width : (i + 1) * width, :] for i in range(len(offsets))]
            place(blocks, [o ^ bit for o in offsets], work_ref, 0)
        out_ref[k] = work_ref[...].T + corr * vec_ref[k, 0:1, :]


def own_matrices(offsets, vec_ref, corr_ref, mine_ref, mate_ref, matrix_ref, psi_ref, work_ref):
    matrices_of(offsets, vec_ref, corr_ref[...], mine_ref, mate_ref, work_ref, matrix_ref)
    psi_ref[0] = matrix_ref[0]
    for k in range(1, matrix_ref.shape[0]):
        psi_ref[k] = dot_nn(matrix_ref[k], psi_ref[k - 1])


def other_matrices(
    offsets, vec_ref, corr_ref, mine_ref, mate_ref, psi_ref, matrix_ref, psi_other_ref, psi_half_ref, work_ref
):
    steps, half, states = mine_ref.shape
    seg = lax.axis_index("seg")
    is_second = lax.rem(seg, 2) == 1
    matrices_of(offsets, vec_ref, corr_ref[...], mine_ref, mate_ref, work_ref, matrix_ref)
    mine = pl.ds(pl.multiple_of(lax.rem(lax.axis_index("col"), 2) * half, 8), half)

    @pl.when(seg < 2)
    def _():
        psi_half_ref[...] = jnp.zeros_like(psi_half_ref)

    @pl.when(seg >= 2)
    def _():
        psi_other_ref[...] = matrix_ref[0]
        for k in range(1, steps):
            psi_other_ref[...] = dot_nn(matrix_ref[k], psi_other_ref[...])

        @pl.when(is_second)
        def _():
            psi_half_ref[...] = dot_nn(psi_ref[steps - 1, mine, :], psi_other_ref[...])

        @pl.when(jnp.logical_not(is_second))
        def _():
            psi_half_ref[...] = dot_nn(psi_other_ref[mine, :], psi_ref[steps - 1])


def put_packed(step_ref, covar, mean, blocks, out_ref):
    states = covar.shape[0]
    edge = states // 3
    core = lax.rem(lax.axis_index("col"), 2)

    @pl.when(core == 0)
    def _():
        rows = step_ref[: 2 * edge, :]
        low = dot_nt(dot_nn(rows, covar), rows)
        out_ref[:edge, :] = low[:edge, :edge] + blocks(0, 0)
        out_ref[edge : 2 * edge, :] = low[edge:, :edge] + blocks(1, 0)
        out_ref[2 * edge : 3 * edge, :] = low[edge:, edge:] + blocks(1, 1)
        out_ref[3 * edge :, :] = jnp.zeros((8, edge), F32)

    @pl.when(core == 1)
    def _():
        rows = step_ref[2 * edge :, :]
        both = dot_nt(jnp.concatenate([dot_nn(rows, covar), mean], axis=0), step_ref[...])
        out_ref[3 * edge :, :] = jnp.zeros((8, edge), F32)
        for j in range(3):
            at = slice(j * edge, (j + 1) * edge)
            out_ref[at, :] = both[:edge, at] + blocks(2, j)
            out_ref[3 * edge + j : 3 * edge + j + 1, :] = both[edge : edge + 1, at] + blocks(3, j)


def unpacked(mine_ref, mate_ref, covar_ref):
    states = covar_ref.shape[0]
    edge = states // 3
    is_low = lax.rem(lax.axis_index("col"), 2) == 0
    low = jnp.where(is_low, mine_ref[...], mate_ref[...])
    high = jnp.where(is_low, mate_ref[...], mine_ref[...])

    def put(i, j, block):
        covar_ref[i * edge : (i + 1) * edge, j * edge : (j + 1) * edge] = block
        if i != j:
            covar_ref[j * edge : (j + 1) * edge, i * edge : (i + 1) * edge] = block.T

    put(0, 0, low[:edge])
    put(1, 0, low[edge : 2 * edge])
    put(1, 1, low[2 * edge : 3 * edge])
    for j in range(3):
        put(2, j, high[j * edge : (j + 1) * edge])
    row = jnp.concatenate([high[3 * edge + j : 3 * edge + j + 1] for j in range(3)], axis=1)
    return mean_block(row, states)


def pair_covariance(
    steps, noise_ref, offset_ref, prior_ref, start_ref, matrix_ref, psi_ref, matrix_other_ref,
    covar_ref, mean_ref, covar_other_ref, mean_other_ref, out_ref, step_ref,
):
    states = prior_ref.shape[0]
    edge = states // 3
    seg = lax.axis_index("seg")
    is_second = lax.rem(seg, 2) == 1
    last = steps - 1
    covar_ref[0] = noise_ref[0]
    mean_ref[0] = offset_ref[0]

    def with_prior(step):
        return square(step, prior_ref[...], mean_block(start_ref[...], states))

    @pl.when(seg == 0)
    def _():
        covar, mean = with_prior(matrix_ref[0])
        covar_ref[0] += covar
        mean_ref[0] += mean

    for k in range(1, steps):
        covar, mean = square(matrix_ref[k], covar_ref[k - 1], mean_ref[k - 1])
        covar_ref[k] = covar + noise_ref[k]
        mean_ref[k] = mean + offset_ref[k]

    @pl.when(is_second)
    def _():
        covar_other_ref[...] = noise_ref[steps]
        mean_other_ref[...] = offset_ref[steps]
        step_ref[...] = psi_ref[last]

        @pl.when(seg == 1)
        def _():
            covar, mean = with_prior(matrix_other_ref[0])
            covar_other_ref[...] += covar
            mean_other_ref[...] += mean

    @pl.when(jnp.logical_not(is_second))
    def _():
        covar_other_ref[...] = covar_ref[last]
        mean_other_ref[...] = mean_ref[last]
        step_ref[...] = matrix_other_ref[last]

    def one_step(k):
        covar, mean = square(matrix_other_ref[k], covar_other_ref[...], mean_other_ref[...])
        covar_other_ref[...] = covar + noise_ref[steps + k]
        mean_other_ref[...] = mean + offset_ref[steps + k]

    for k in range(last):
        one_step(k + is_second.astype(jnp.int32))

    def blocks(i, j):
        at = slice(j * edge, (j + 1) * edge)
        if i == 3:
            return jnp.where(is_second, mean_ref[last, :1, at], offset_ref[steps + last, :1, at])
        rows = slice(i * edge, (i + 1) * edge)
        return jnp.where(is_second, covar_ref[last, rows, at], noise_ref[steps + last, rows, at])

    put_packed(step_ref, covar_other_ref[...], mean_other_ref[...], blocks, out_ref)


def pair_elements(steps, width, psi_ref, covar_ref, mean_ref, psi_other_ref, covar_other_ref, mean_other_ref, *refs):
    psi_out_ref, covar_out_ref, mean_out_ref, psi_all_ref = refs
    seg = lax.axis_index("seg")
    is_second = lax.rem(seg, 2) == 1
    mine = pl.ds(pl.multiple_of(lax.axis_index("col") * width, 8), width)

    @pl.when(seg < 2)
    def _():
        psi_out_ref[...] = jnp.zeros_like(psi_out_ref)
        psi_all_ref[...] = jnp.zeros_like(psi_all_ref)

    @pl.when(seg >= 2)
    def _():
        for k in range(steps):

            @pl.when(is_second)
            def _():
                psi_out_ref[k] = dot_nn(psi_ref[k], psi_other_ref[...])

            @pl.when(jnp.logical_not(is_second))
            def _():
                psi_out_ref[k] = psi_ref[k]

        @pl.when(is_second)
        def _():
            psi_all_ref[...] = psi_out_ref[steps - 1]

        @pl.when(jnp.logical_not(is_second))
        def _():
            psi_all_ref[...] = dot_nn(psi_other_ref[...], psi_ref[steps - 1])

    @pl.when(is_second)
    def _():
        covar, mean = covar_other_ref[...], mean_other_ref[...]
        for k in range(steps):
            half = dot_nn(psi_ref[k, mine, :], covar)
            both = dot_nt(jnp.concatenate([half, mean], axis=0), psi_ref[k])
            covar_out_ref[k] = both[:width] + covar_ref[k, mine, :]
            mean_out_ref[k] = both[width:] + mean_ref[k]

    @pl.when(jnp.logical_not(is_second))
    def _():
        for k in range(steps):
            covar_out_ref[k] = covar_ref[k, mine, :]
            mean_out_ref[k] = mean_ref[k]


def packed_blocks(ref, edge):
    def blocks(i, j):
        if i == 3:
            return ref[3 * edge + j : 3 * edge + j + 1, :]
        at = (i + j) if i < 2 else j
        return ref[at * edge : (at + 1) * edge, :]

    return blocks


def whole_matrix(mine_ref, mate_ref):
    is_low = lax.rem(lax.axis_index("col"), 2) == 0
    mine, mate = mine_ref[...], mate_ref[...]
    return jnp.concatenate([jnp.where(is_low, mine, mate), jnp.where(is_low, mate, mine)], axis=0)


def is_upper(bit):
    return lax.rem(lax.div(lax.axis_index("seg"), bit), 2) == 1


def joined_covariance(
    bit, last, psi_ref, mine_ref, mate_ref, step_mine_ref, step_mate_ref, came_mine_ref, came_mate_ref, out_ref,
    step_ref, first_mine_ref, first_mate_ref, added_ref, work_ref,
):
    @pl.when(jnp.logical_not(last) | jnp.logical_not(is_upper(2 * bit)))
    def _():
        upper = is_upper(bit)
        step_ref[...] = jnp.where(upper, psi_ref[...], whole_matrix(step_mine_ref, step_mate_ref))
        first_mine_ref[...] = jnp.where(upper, came_mine_ref[...], mine_ref[...])
        first_mate_ref[...] = jnp.where(upper, came_mate_ref[...], mate_ref[...])
        added_ref[...] = jnp.where(upper, mine_ref[...], came_mine_ref[...])
        mean = unpacked(first_mine_ref, first_mate_ref, work_ref)
        put_packed(step_ref, work_ref[...], mean, packed_blocks(added_ref, out_ref.shape[1]), out_ref)


def joined_matrix(bit, psi_ref, step_mine_ref, step_mate_ref, out_ref):
    came = whole_matrix(step_mine_ref, step_mate_ref)
    upper = is_upper(bit)
    out_ref[...] = dot_nn(jnp.where(upper, psi_ref[...], came), jnp.where(upper, came, psi_ref[...]))


def entered(bit, psi_ref, covar_ref, mean_ref, step_mine_ref, step_mate_ref, mine_ref, mate_ref, *refs):
    psi_out_ref, covar_out_ref, mean_out_ref, work_ref = refs
    steps, width, states = covar_ref.shape
    mine = pl.ds(pl.multiple_of(lax.axis_index("col") * width, 8), width)

    @pl.when(is_upper(bit))
    def _():
        before = whole_matrix(step_mine_ref, step_mate_ref)
        mean = unpacked(mine_ref, mate_ref, work_ref)
        covar = work_ref[...]
        for k in range(steps):
            psi_out_ref[k] = dot_nn(psi_ref[k], before)
            half = dot_nn(psi_ref[k, mine, :], covar)
            both = dot_nt(jnp.concatenate([half, mean], axis=0), psi_ref[k])
            covar_out_ref[k] = both[:width] + covar_ref[k]
            mean_out_ref[k] = both[width:] + mean_ref[k]

    @pl.when(jnp.logical_not(is_upper(bit)))
    def _():
        psi_out_ref[...] = psi_ref[...]
        covar_out_ref[...] = covar_ref[...]
        mean_out_ref[...] = mean_ref[...]


def finished(bit, psi_ref, covar_ref, mean_ref, mine_ref, mate_ref, covar_out_ref, mean_out_ref, work_ref):
    steps, width, states = covar_ref.shape
    mine = pl.ds(pl.multiple_of(lax.axis_index("col") * width, 8), width)

    @pl.when(is_upper(bit))
    def _():
        mean = unpacked(mine_ref, mate_ref, work_ref)
        rows = jnp.concatenate([psi_ref[k, mine, :] for k in range(steps)], axis=0)
        half = dot_nn(rows, work_ref[...])
        for k in range(steps):
            part = half[k * width : (k + 1) * width]
            both = dot_nt(jnp.concatenate([part, mean], axis=0), psi_ref[k])
            covar_out_ref[k] = both[:width] + covar_ref[k]
            mean_out_ref[k : k + 1, :] = both[width : width + 1] + mean_ref[k, :1, :]

    @pl.when(jnp.logical_not(is_upper(bit)))
    def _():
        covar_out_ref[...] = covar_ref[...]
        for k in range(steps):
            mean_out_ref[k : k + 1, :] = mean_ref[k, :1, :]


def swapped(block, axis, bit):
    return lax.ppermute(block, axis, [(i, i ^ bit) for i in range(lax.axis_size(axis))])


def with_mate(share):
    return (share, swapped(share, "col", 1))


def per_device(
    model_mixing,
    retention,
    forcing,
    observations,
    model_noise,
    obs_noise,
    gain,
    obs_operator_t,
    prior_mean,
    prior_factor,
):
    steps, width, states = model_mixing.shape
    n_col, n_seg = lax.axis_size("col"), lax.axis_size("seg")
    col = lax.axis_index("col")
    edge = states // 3
    square_shape, mean_shape = (states, states), (MEAN_ROWS, states)
    share_shape, half_shape = (3 * edge + 8, edge), (states // 2, states)
    far_bits = []
    bit = n_col // 2
    while bit > 1:
        far_bits.append(bit)
        bit //= 2
    offsets = [0]
    for bit in far_bits:
        offsets = offsets + [o ^ bit for o in offsets]

    own = [model_mixing]
    for bit in far_bits:
        own = own + [swapped(b, "col", bit) for b in own]
    near = swapped(model_mixing, "seg", 1)
    corr_mine, vectors = local_call(
        correction_rows,
        [(width, states), (steps, 4, states)],
        gain,
        obs_operator_t,
        observations,
        retention,
        forcing,
        model_noise,
        copied=True,
        cost=3,
    )
    corr = [corr_mine]
    for bit in far_bits:
        corr = corr + [swapped(b, "col", bit) for b in corr]
    vectors_other = swapped(vectors, "seg", 1)
    fixed, prior = local_call(
        fixed_parts, [square_shape, square_shape], gain, obs_noise[None, :], prior_factor
    )
    own, near, fixed, vectors_other = lax.optimization_barrier((own, near, fixed, vectors_other))
    other = [near] + [swapped(b, "seg", 1) for b in own[1:]]
    corr, vectors_other, fixed = lax.optimization_barrier((corr, vectors_other, fixed))
    corr = corr + [swapped(b, "col", 1) for b in corr]

    rows_shape = (steps,) + half_shape
    correction, rows = local_call(
        functools.partial(own_rows, offsets + [o ^ 1 for o in offsets]),
        [square_shape, rows_shape],
        *corr,
        *own,
        scratch=[square_shape],
    )
    noise, offset = local_call(
        noises,
        [(2 * steps,) + square_shape, (2 * steps,) + mean_shape],
        vectors,
        vectors_other,
        fixed,
        correction,
    )
    other, correction, noise = lax.optimization_barrier((other, correction, noise))
    rows = with_mate(rows)
    (rows_other,) = local_call(other_rows, [rows_shape], correction, *other, cost=1)
    matrix, psi = local_call(
        functools.partial(own_matrices, offsets),
        [(steps,) + square_shape, (steps,) + square_shape],
        vectors,
        correction,
        *rows,
        scratch=[square_shape],
        cost=1,
    )
    matrix_other, psi_other, psi_half = local_call(
        functools.partial(other_matrices, offsets),
        [(steps,) + square_shape, square_shape, half_shape],
        vectors_other,
        correction,
        *with_mate(rows_other),
        psi,
        scratch=[square_shape],
    )
    bit = 2
    more = 2 * bit < n_seg
    if more:
        step = swapped(psi_half, "seg", bit)
    covar, mean, covar_other, mean_other, total = local_call(
        functools.partial(pair_covariance, steps),
        [(steps,) + square_shape, (steps,) + mean_shape, square_shape, mean_shape, share_shape],
        noise,
        offset,
        prior,
        prior_mean[None, :],
        matrix,
        psi,
        matrix_other,
        scratch=[square_shape],
    )
    came = swapped(total, "seg", bit)
    psi, covar, mean, psi_all = local_call(
        functools.partial(pair_elements, steps, width),
        [(steps,) + square_shape, (steps, width, states), (steps,) + mean_shape, square_shape],
        psi,
        covar,
        mean,
        psi_other,
        covar_other,
        mean_other,
    )
    while more:
        total = with_mate(total)
        came, step, psi_all, psi = lax.optimization_barrier((came, step, psi_all, psi))
        came, step = with_mate(came), with_mate(step)
        last = 4 * bit >= n_seg
        (total_next,) = local_call(
            functools.partial(joined_covariance, bit, last),
            [share_shape],
            psi_all,
            *total,
            *step,
            *came,
            scratch=[square_shape, share_shape, share_shape, share_shape, square_shape],
        )
        came_next = swapped(total_next, "seg", 2 * bit)
        psi, covar, mean = local_call(
            functools.partial(entered, bit),
            [(steps,) + square_shape, (steps, width, states), (steps,) + mean_shape],
            psi,
            covar,
            mean,
            *step,
            *came,
            scratch=[square_shape],
        )
        if not last:
            (psi_all,) = local_call(functools.partial(joined_matrix, bit), [square_shape], psi_all, *step)
            psi_half = lax.dynamic_slice_in_dim(psi_all, col % 2 * (states // 2), states // 2, 0)
            step = swapped(psi_half, "seg", 2 * bit)
        total, came = total_next, came_next
        bit *= 2
        more = not last
    came, psi = lax.optimization_barrier((came, psi))
    covars, means = local_call(
        functools.partial(finished, bit),
        [(steps, width, states), (steps, states)],
        psi,
        covar,
        mean,
        *with_mate(came),
        scratch=[square_shape],
    )
    return means, covars


def solution(mesh):
    in_specs = (
        P("seg", "col", None),
        P("seg", None),
        P("seg", None),
        P("seg", None),
        P("seg", None),
        P(),
        P(),
        P("col", None),
        P(),
        P(),
    )
    out_specs = (P("seg", None), P("seg", "col", None))
    return jax.shard_map(
        per_device, mesh=mesh, in_specs=in_specs, out_specs=out_specs, check_vma=False
    )
```

```python
import functools

import jax
import jax.numpy as jnp
from jax import lax
from jax.experimental import pallas as pl
from jax.experimental.pallas import tpu as pltpu
from jax.sharding import PartitionSpec as P

F32, BF16 = jnp.float32, jnp.bfloat16
NN = (((1,), (0,)), ((), ()))
NT = (((1,), (1,)), ((), ()))
MEAN_ROWS = 16
CHUNKS = 4
COST = 7 * 10**8


def parts(x):
    high = x.astype(BF16)
    return high, (x - high.astype(F32)).astype(BF16)


def as_left(x):
    high, low = parts(x)
    return jnp.concatenate([high, high, low], axis=1)


def as_right(x, axis):
    high, low = parts(x)
    return jnp.concatenate([high, low, high], axis=axis)


def dot_nn(left, right):
    return lax.dot_general(as_left(left), as_right(right, 0), NN, preferred_element_type=F32)


def dot_nt(left, right):
    return lax.dot_general(as_left(left), as_right(right, 1), NT, preferred_element_type=F32)


def square(step, covar, mean):
    rows = covar.shape[0]
    both = dot_nt(jnp.concatenate([dot_nn(step, covar), mean], axis=0), step)
    return both[:rows], both[rows:]


def mean_block(row, states):
    return jnp.broadcast_to(row, (MEAN_ROWS, states))


def local_call(body, outs, *operands, scratch=(), copied=False, cost=0):
    shapes = [jax.ShapeDtypeStruct(shape, F32) for shape in outs]
    return pl.pallas_call(
        body,
        out_shape=shapes,
        name=getattr(body, "func", body).__name__,
        in_specs=[pl.BlockSpec(memory_space=pltpu.HBM if copied else pltpu.VMEM)] * len(operands),
        scratch_shapes=[pltpu.VMEM(o.shape, F32) for o in operands if copied]
        + [pltpu.SemaphoreType.DMA((len(operands) + CHUNKS,))] * copied
        + [pltpu.VMEM(shape, F32) for shape in scratch],
        compiler_params=pltpu.CompilerParams(vmem_limit_bytes=(58 if copied else 36) * 2**20),
        cost_estimate=pl.CostEstimate(
            flops=cost * COST, bytes_accessed=4096, transcendentals=0
        ),
    )(*operands)


def by_gain(left, right):
    return lax.dot_general(as_left(left), right, NT, preferred_element_type=F32)


def correction_rows(
    gain_hbm, oper_hbm, seen_hbm, keep_hbm, push_hbm, var_hbm, corr_ref, vec_ref,
    gain_ref, oper_ref, seen_ref, keep_ref, push_ref, var_ref, sems,
):
    width, states = corr_ref.shape
    steps = keep_ref.shape[0]
    observed = gain_hbm.shape[1]
    chunk = observed // CHUNKS
    pairs = [
        (oper_hbm, oper_ref),
        (seen_hbm, seen_ref),
        (keep_hbm, keep_ref),
        (push_hbm, push_ref),
        (var_hbm, var_ref),
    ]
    small = [pltpu.make_async_copy(a, b, sems.at[i]) for i, (a, b) in enumerate(pairs)]
    large = []
    for i in range(CHUNKS):
        at = pl.ds(i * chunk, chunk)
        large.append(pltpu.make_async_copy(gain_hbm.at[:, at], gain_ref.at[:, at], sems.at[len(pairs) + i]))
    for move in small[:2] + large + small[2:]:
        move.start()
    rows = lax.broadcasted_iota(jnp.int32, (width, states), 0) + lax.axis_index("col") * width
    cols = lax.broadcasted_iota(jnp.int32, (width, states), 1)
    small[0].wait()
    small[1].wait()
    blank = jnp.zeros((MEAN_ROWS - steps, observed), F32)
    left = jnp.concatenate([oper_ref[...], seen_ref[...], blank], axis=0)
    both = None
    for i in range(CHUNKS):
        at = slice(i * chunk, (i + 1) * chunk)
        large[i].wait()
        part = dot_nt(left[:, at], gain_ref[:, at])
        both = part if both is None else both + part
    corr_ref[...] = (rows == cols).astype(F32) - both[:width]
    for move in small[2:]:
        move.wait()
    for k in range(steps):
        here = slice(k, k + 1)
        vec_ref[k, 0:1, :] = keep_ref[here, :]
        vec_ref[k, 1:2, :] = var_ref[here, :]
        vec_ref[k, 2:3, :] = push_ref[here, :]
        vec_ref[k, 3:4, :] = both[width + k : width + k + 1]


def fixed_parts(gain_ref, noise_ref, factor_ref, fixed_ref, prior_ref):
    gain = gain_ref[...]
    fixed_ref[...] = by_gain(gain * noise_ref[...], as_right(gain, 1))

    @pl.when(lax.axis_index("seg") < 2)
    def _():
        prior_ref[...] = dot_nt(factor_ref[...], factor_ref[...])


def place(pieces, offsets, out_ref, base):
    me = lax.axis_index("col")
    width = pieces[0].shape[-2]
    for piece, offset in zip(pieces, offsets):
        at = pl.multiple_of((me ^ offset) * width + base, 8)
        out_ref[pl.ds(at, width), :] = piece


def noises(vec_ref, fixed_ref, corr_ref, noise_ref, offset_ref):
    steps, states = vec_ref.shape[0], corr_ref.shape[0]
    corr = corr_ref[...]
    vectors = [vec_ref[k] for k in range(steps)]
    push = [v[2:3] for v in vectors] + [jnp.zeros((MEAN_ROWS - steps, states), F32)]
    left = jnp.concatenate([corr * v[1:2] for v in vectors] + push, axis=0)
    both = dot_nt(left, corr)
    base = steps * states
    for k in range(steps):
        noise_ref[k] = both[k * states : (k + 1) * states] + fixed_ref[...]
        offset_ref[k] = mean_block(both[base + k : base + k + 1] + vectors[k][3:4], states)


def mixed_rows(out_ref, pieces, corr):
    steps, width = pieces[0].shape[:2]
    rows = jnp.concatenate([piece[k] for k in range(steps) for piece in pieces], axis=0)
    mixed = dot_nt(rows, corr)
    half = width * len(pieces)
    for k in range(steps):
        out_ref[k] = mixed[k * half : (k + 1) * half]


def own_rows(offsets, *refs):
    n_piece = len(offsets)
    pieces, own, (corr_ref, out_ref, work_ref) = refs[:n_piece], refs[n_piece:-3], refs[-3:]
    place([p[...] for p in pieces], offsets, work_ref, 0)
    corr_ref[...] = work_ref[...].T
    mixed_rows(out_ref, own, corr_ref[...])


def other_rows(corr_ref, *refs):
    mixed_rows(refs[-1], refs[:-1], corr_ref[...])


def matrices_of(offsets, vec_ref, corr, mine_ref, mate_ref, work_ref, out_ref):
    steps, half, states = mine_ref.shape
    width = half // len(offsets)
    for k in range(steps):
        for ref, bit in ((mine_ref, 0), (mate_ref, 1)):
            blocks = [ref[k, i * width : (i + 1) * width, :] for i in range(len(offsets))]
            place(blocks, [o ^ bit for o in offsets], work_ref, 0)
        out_ref[k] = work_ref[...].T + corr * vec_ref[k, 0:1, :]


def add_prior(step_ref, prior_ref, start_ref, covar_ref, mean_ref):
    covar, mean = square(step_ref[0], prior_ref[...], mean_block(start_ref[...], prior_ref.shape[0]))
    covar_ref[...] += covar
    mean_ref[...] += mean


def own_segment(
    offsets, vec_ref, corr_ref, mine_ref, mate_ref, noise_ref, offset_ref, prior_ref, start_ref,
    matrix_ref, psi_ref, covar_ref, mean_ref, work_ref,
):
    steps = matrix_ref.shape[0]
    matrices_of(offsets, vec_ref, corr_ref[...], mine_ref, mate_ref, work_ref, matrix_ref)
    covar_ref[0] = noise_ref[0]
    mean_ref[0] = offset_ref[0]

    @pl.when(lax.axis_index("seg") == 0)
    def _():
        add_prior(matrix_ref, prior_ref, start_ref, covar_ref.at[0], mean_ref.at[0])

    psi_ref[0] = matrix_ref[0]
    for k in range(1, steps):
        psi_ref[k] = dot_nn(matrix_ref[k], psi_ref[k - 1])
        covar, mean = square(matrix_ref[k], covar_ref[k - 1], mean_ref[k - 1])
        covar_ref[k] = covar + noise_ref[k]
        mean_ref[k] = mean + offset_ref[k]


def other_matrices(
    offsets, vec_ref, corr_ref, mine_ref, mate_ref, psi_ref, prior_ref, start_ref,
    matrix_ref, psi_other_ref, psi_half_ref, covar_ref, mean_ref, work_ref,
):
    steps, half, states = mine_ref.shape
    seg = lax.axis_index("seg")
    is_second = lax.rem(seg, 2) == 1
    matrices_of(offsets, vec_ref, corr_ref[...], mine_ref, mate_ref, work_ref, matrix_ref)
    mine = pl.ds(pl.multiple_of(lax.rem(lax.axis_index("col"), 2) * half, 8), half)
    covar_ref[...] = jnp.zeros_like(covar_ref)
    mean_ref[...] = jnp.zeros_like(mean_ref)

    @pl.when(seg == 1)
    def _():
        add_prior(matrix_ref, prior_ref, start_ref, covar_ref, mean_ref)

    @pl.when(seg < 2)
    def _():
        psi_half_ref[...] = jnp.zeros_like(psi_half_ref)

    @pl.when(seg >= 2)
    def _():
        psi_other_ref[...] = matrix_ref[0]
        for k in range(1, steps):
            psi_other_ref[...] = dot_nn(matrix_ref[k], psi_other_ref[...])

        @pl.when(is_second)
        def _():
            psi_half_ref[...] = dot_nn(psi_ref[steps - 1, mine, :], psi_other_ref[...])

        @pl.when(jnp.logical_not(is_second))
        def _():
            psi_half_ref[...] = dot_nn(psi_other_ref[mine, :], psi_ref[steps - 1])


def put_packed(step_ref, covar, mean, blocks, out_ref):
    states = covar.shape[0]
    edge = states // 3
    core = lax.rem(lax.axis_index("col"), 2)

    @pl.when(core == 0)
    def _():
        rows = step_ref[: 2 * edge, :]
        low = dot_nt(dot_nn(rows, covar), rows)
        out_ref[:edge, :] = low[:edge, :edge] + blocks(0, 0)
        out_ref[edge : 2 * edge, :] = low[edge:, :edge] + blocks(1, 0)
        out_ref[2 * edge : 3 * edge, :] = low[edge:, edge:] + blocks(1, 1)
        out_ref[3 * edge :, :] = jnp.zeros((8, edge), F32)

    @pl.when(core == 1)
    def _():
        rows = step_ref[2 * edge :, :]
        both = dot_nt(jnp.concatenate([dot_nn(rows, covar), mean], axis=0), step_ref[...])
        out_ref[3 * edge :, :] = jnp.zeros((8, edge), F32)
        for j in range(3):
            at = slice(j * edge, (j + 1) * edge)
            out_ref[at, :] = both[:edge, at] + blocks(2, j)
            out_ref[3 * edge + j : 3 * edge + j + 1, :] = both[edge : edge + 1, at] + blocks(3, j)


def unpacked(mine_ref, mate_ref, covar_ref):
    states = covar_ref.shape[0]
    edge = states // 3
    is_low = lax.rem(lax.axis_index("col"), 2) == 0
    low = jnp.where(is_low, mine_ref[...], mate_ref[...])
    high = jnp.where(is_low, mate_ref[...], mine_ref[...])

    def put(i, j, block):
        covar_ref[i * edge : (i + 1) * edge, j * edge : (j + 1) * edge] = block
        if i != j:
            covar_ref[j * edge : (j + 1) * edge, i * edge : (i + 1) * edge] = block.T

    put(0, 0, low[:edge])
    put(1, 0, low[edge : 2 * edge])
    put(1, 1, low[2 * edge : 3 * edge])
    for j in range(3):
        put(2, j, high[j * edge : (j + 1) * edge])
    row = jnp.concatenate([high[3 * edge + j : 3 * edge + j + 1] for j in range(3)], axis=1)
    return mean_block(row, states)


def pair_covariance(
    steps, psi_ref, covar_ref, mean_ref, noise_other_ref, offset_other_ref, matrix_other_ref, first_other_ref,
    first_mean_other_ref, covar_other_ref, mean_other_ref, out_ref, step_ref,
):
    states = first_other_ref.shape[0]
    edge = states // 3
    is_second = lax.rem(lax.axis_index("seg"), 2) == 1
    last = steps - 1

    @pl.when(is_second)
    def _():
        covar_other_ref[...] = noise_other_ref[0] + first_other_ref[...]
        mean_other_ref[...] = offset_other_ref[0] + first_mean_other_ref[...]
        step_ref[...] = psi_ref[last]

    @pl.when(jnp.logical_not(is_second))
    def _():
        covar_other_ref[...] = covar_ref[last]
        mean_other_ref[...] = mean_ref[last]
        step_ref[...] = matrix_other_ref[last]

    for k in range(last):
        at = k + is_second.astype(jnp.int32)
        covar, mean = square(matrix_other_ref[at], covar_other_ref[...], mean_other_ref[...])
        covar_other_ref[...] = covar + noise_other_ref[at]
        mean_other_ref[...] = mean + offset_other_ref[at]

    def blocks(i, j):
        at = slice(j * edge, (j + 1) * edge)
        if i == 3:
            return jnp.where(is_second, mean_ref[last, :1, at], offset_other_ref[last, :1, at])
        rows = slice(i * edge, (i + 1) * edge)
        return jnp.where(is_second, covar_ref[last, rows, at], noise_other_ref[last, rows, at])

    put_packed(step_ref, covar_other_ref[...], mean_other_ref[...], blocks, out_ref)


def pair_elements(steps, width, psi_ref, covar_ref, mean_ref, psi_other_ref, covar_other_ref, mean_other_ref, *refs):
    psi_out_ref, covar_out_ref, mean_out_ref, psi_all_ref = refs
    seg = lax.axis_index("seg")
    is_second = lax.rem(seg, 2) == 1
    mine = pl.ds(pl.multiple_of(lax.axis_index("col") * width, 8), width)

    @pl.when(seg < 2)
    def _():
        psi_out_ref[...] = jnp.zeros_like(psi_out_ref)
        psi_all_ref[...] = jnp.zeros_like(psi_all_ref)

    @pl.when(seg >= 2)
    def _():
        for k in range(steps):

            @pl.when(is_second)
            def _():
                psi_out_ref[k] = dot_nn(psi_ref[k], psi_other_ref[...])

            @pl.when(jnp.logical_not(is_second))
            def _():
                psi_out_ref[k] = psi_ref[k]

        @pl.when(is_second)
        def _():
            psi_all_ref[...] = psi_out_ref[steps - 1]

        @pl.when(jnp.logical_not(is_second))
        def _():
            psi_all_ref[...] = dot_nn(psi_other_ref[...], psi_ref[steps - 1])

    @pl.when(is_second)
    def _():
        covar, mean = covar_other_ref[...], mean_other_ref[...]
        for k in range(steps):
            half = dot_nn(psi_ref[k, mine, :], covar)
            both = dot_nt(jnp.concatenate([half, mean], axis=0), psi_ref[k])
            covar_out_ref[k] = both[:width] + covar_ref[k, mine, :]
            mean_out_ref[k] = both[width:] + mean_ref[k]

    @pl.when(jnp.logical_not(is_second))
    def _():
        for k in range(steps):
            covar_out_ref[k] = covar_ref[k, mine, :]
            mean_out_ref[k] = mean_ref[k]


def packed_blocks(ref, edge):
    def blocks(i, j):
        if i == 3:
            return ref[3 * edge + j : 3 * edge + j + 1, :]
        at = (i + j) if i < 2 else j
        return ref[at * edge : (at + 1) * edge, :]

    return blocks


def whole_matrix(mine_ref, mate_ref):
    is_low = lax.rem(lax.axis_index("col"), 2) == 0
    mine, mate = mine_ref[...], mate_ref[...]
    return jnp.concatenate([jnp.where(is_low, mine, mate), jnp.where(is_low, mate, mine)], axis=0)


def place_in(bit):
    return lax.div(lax.rem(lax.axis_index("seg"), 2 * bit) - bit, 2) - (lax.rem(lax.axis_index("seg"), 2 * bit) < bit)


def is_upper(bit):
    return lax.rem(lax.axis_index("seg"), 2 * bit) >= bit


def chosen(refs, bit):
    at = place_in(bit)
    value = refs[0][...]
    for i, ref in enumerate(refs[1:]):
        value = jnp.where(at == i + 1, ref[...], value)
    return value


def joined_covariance(bit, psi_ref, total_ref, *refs):
    n_group = bit // 2
    mines, mates = refs[:n_group], refs[n_group : 2 * n_group]
    out_ref, mine_ref, mate_ref, work_ref = refs[2 * n_group :]

    @pl.when(lax.rem(lax.axis_index("seg"), 2 * bit) >= 2 * bit - 2)
    def _():
        mine_ref[...] = chosen(mines, bit)
        mate_ref[...] = chosen(mates, bit)
        mean = unpacked(mine_ref, mate_ref, work_ref)
        put_packed(psi_ref, work_ref[...], mean, packed_blocks(total_ref, out_ref.shape[1]), out_ref)


def joined_matrix(bit, psi_ref, *refs):
    n_group = bit // 2
    psi_ref_out, mine_ref, mate_ref = refs[2 * n_group :]
    mine_ref[...] = chosen(refs[:n_group], bit)
    mate_ref[...] = chosen(refs[n_group : 2 * n_group], bit)
    psi_ref_out[...] = dot_nn(psi_ref[...], whole_matrix(mine_ref, mate_ref))


def entered(bit, psi_ref, covar_ref, mean_ref, *refs):
    n_group = bit // 2
    mines, mates = refs[:n_group], refs[n_group : 2 * n_group]
    covar_out_ref, mean_out_ref, mine_ref, mate_ref, work_ref = refs[2 * n_group :]
    steps, width, states = covar_ref.shape
    mine = pl.ds(pl.multiple_of(lax.axis_index("col") * width, 8), width)

    @pl.when(is_upper(bit))
    def _():
        mine_ref[...] = chosen(mines, bit)
        mate_ref[...] = chosen(mates, bit)
        mean = unpacked(mine_ref, mate_ref, work_ref)
        covar = work_ref[...]
        for k in range(steps):
            half = dot_nn(psi_ref[k, mine, :], covar)
            both = dot_nt(jnp.concatenate([half, mean], axis=0), psi_ref[k])
            covar_out_ref[k] = both[:width] + covar_ref[k]
            mean_out_ref[k] = both[width:] + mean_ref[k]

    @pl.when(jnp.logical_not(is_upper(bit)))
    def _():
        covar_out_ref[...] = covar_ref[...]
        mean_out_ref[...] = mean_ref[...]


def takes_matrix(bit):
    return is_upper(bit) & (lax.axis_index("seg") >= 2 * bit)


def matrices_entered(bit, psi_ref, *refs):
    n_group = bit // 2
    psi_out_ref, mine_ref, mate_ref = refs[2 * n_group :]
    psi_out_ref[...] = psi_ref[...]

    @pl.when(takes_matrix(bit))
    def _():
        mine_ref[...] = chosen(refs[:n_group], bit)
        mate_ref[...] = chosen(refs[n_group : 2 * n_group], bit)
        before = whole_matrix(mine_ref, mate_ref)
        for k in range(psi_ref.shape[0]):
            psi_out_ref[k] = dot_nn(psi_ref[k], before)


def finished(bit, n_step, psi_ref, covar_ref, mean_ref, *refs):
    n_group = bit // 2
    step_refs, refs = refs[: 2 * n_step], refs[2 * n_step :]
    mines, mates = refs[:n_group], refs[n_group : 2 * n_group]
    covar_out_ref, mean_out_ref, mine_ref, mate_ref, work_ref, half_ref, other_half_ref, rows_ref, enter_ref = refs[2 * n_group :]
    steps, width, states = covar_ref.shape
    mine = pl.ds(pl.multiple_of(lax.axis_index("col") * width, 8), width)

    @pl.when(is_upper(bit))
    def _():
        mine_ref[...] = chosen(mines, bit)
        mate_ref[...] = chosen(mates, bit)
        mean = unpacked(mine_ref, mate_ref, work_ref)
        for k in range(steps):
            rows_ref[k * width : (k + 1) * width, :] = psi_ref[k, mine, :]
        n_row = steps * width

        def through(rows):
            return jnp.concatenate([dot_nn(rows, work_ref[...]), mean], axis=0)

        if n_step:

            @pl.when(takes_matrix(bit // 2))
            def _():
                half_ref[...] = chosen(step_refs[:n_step], bit // 2)
                other_half_ref[...] = chosen(step_refs[n_step:], bit // 2)
                before = whole_matrix(half_ref, other_half_ref)
                enter_ref[...] = dot_nt(through(dot_nn(rows_ref[...], before)), before)

            @pl.when(jnp.logical_not(takes_matrix(bit // 2)))
            def _():
                enter_ref[...] = through(rows_ref[...])
        else:
            enter_ref[...] = through(rows_ref[...])
        for k in range(steps):
            part = jnp.concatenate([enter_ref[k * width : (k + 1) * width, :], enter_ref[n_row:, :]], axis=0)
            both = dot_nt(part, psi_ref[k])
            covar_out_ref[k] = both[:width] + covar_ref[k]
            mean_out_ref[k : k + 1, :] = both[width : width + 1] + mean_ref[k, :1, :]

    @pl.when(jnp.logical_not(is_upper(bit)))
    def _():
        covar_out_ref[...] = covar_ref[...]
        for k in range(steps):
            mean_out_ref[k : k + 1, :] = mean_ref[k, :1, :]


def swapped(block, axis, bit):
    return lax.ppermute(block, axis, [(i, i ^ bit) for i in range(lax.axis_size(axis))])


def handed_up(block, bit, first=0):
    n_seg, n_col = lax.axis_size("seg"), lax.axis_size("col")
    came = []
    for group in range(bit // 2):
        aside = n_col // 2 if group % 2 == 0 else n_col
        to = {i: i ^ aside for i in range(n_seg * n_col)}
        for low in range(first * 2 * bit, n_seg, 2 * bit):
            for i in range((low + bit - 2) * n_col, (low + bit) * n_col):
                j = i + (2 + 2 * group) * n_col
                to[i], to[j] = j, i
        came.append(lax.ppermute(block, ("seg", "col"), sorted(to.items())))
    return came


def with_mate(share):
    return (share, swapped(share, "col", 1))


def per_device(
    model_mixing,
    retention,
    forcing,
    observations,
    model_noise,
    obs_noise,
    gain,
    obs_operator_t,
    prior_mean,
    prior_factor,
):
    steps, width, states = model_mixing.shape
    n_col, n_seg = lax.axis_size("col"), lax.axis_size("seg")
    col = lax.axis_index("col")
    edge = states // 3
    square_shape, mean_shape = (states, states), (MEAN_ROWS, states)
    share_shape, half_shape = (3 * edge + 8, edge), (states // 2, states)
    far_bits = []
    bit = n_col // 2
    while bit > 1:
        far_bits.append(bit)
        bit //= 2
    offsets = [0]
    for bit in far_bits:
        offsets = offsets + [o ^ bit for o in offsets]

    own = [model_mixing]
    for bit in far_bits:
        own = own + [swapped(b, "col", bit) for b in own]
    near = swapped(model_mixing, "seg", 1)
    corr_mine, vectors = local_call(
        correction_rows,
        [(width, states), (steps, 4, states)],
        gain,
        obs_operator_t,
        observations,
        retention,
        forcing,
        model_noise,
        copied=True,
        cost=3,
    )
    corr_mine, gain = lax.optimization_barrier((corr_mine, gain))
    fixed, prior = local_call(
        fixed_parts, [square_shape, square_shape], gain, obs_noise[None, :], prior_factor
    )
    corr = [corr_mine]
    for bit in far_bits:
        corr = corr + [swapped(b, "col", bit) for b in corr]
    vectors_other = swapped(vectors, "seg", 1)
    own, near, fixed, vectors_other = lax.optimization_barrier((own, near, fixed, vectors_other))
    other = [near] + [swapped(b, "seg", 1) for b in own[1:]]
    corr = corr + [swapped(b, "col", 1) for b in corr]
    rows_shape = (steps,) + half_shape
    noise_shapes = [(steps,) + square_shape, (steps,) + mean_shape]
    correction, rows = local_call(
        functools.partial(own_rows, offsets + [o ^ 1 for o in offsets]),
        [square_shape, rows_shape],
        *corr,
        *own,
        scratch=[square_shape],
    )
    noise, offset = local_call(noises, noise_shapes, vectors, fixed, correction)
    start = prior_mean[None, :]
    noise_other, offset_other = local_call(noises, noise_shapes, vectors_other, fixed, correction)
    other, correction, noise, noise_other = lax.optimization_barrier((other, correction, noise, noise_other))
    (rows_other,) = local_call(other_rows, [rows_shape], correction, *other)
    matrix, psi, covar, mean = local_call(
        functools.partial(own_segment, offsets),
        [(steps,) + square_shape, (steps,) + square_shape, (steps,) + square_shape, (steps,) + mean_shape],
        vectors,
        correction,
        *with_mate(rows),
        noise,
        offset,
        prior,
        start,
        scratch=[square_shape],
        cost=1,
    )
    matrix_other, psi_other, psi_half, first_other, first_mean_other = local_call(
        functools.partial(other_matrices, offsets),
        [(steps,) + square_shape, square_shape, half_shape, square_shape, mean_shape],
        vectors_other,
        correction,
        *with_mate(rows_other),
        psi,
        prior,
        start,
        scratch=[square_shape],
    )
    bit = 2
    more = 2 * bit < n_seg
    covar_other, mean_other, total = local_call(
        functools.partial(pair_covariance, steps),
        [square_shape, mean_shape, share_shape],
        psi,
        covar,
        mean,
        noise_other,
        offset_other,
        matrix_other,
        first_other,
        first_mean_other,
        scratch=[square_shape],
    )
    total, psi_half = lax.optimization_barrier((total, psi_half))
    came = handed_up(total, bit)
    step = []
    if more:
        step = handed_up(psi_half, bit, 1)
    psi, covar, mean, psi_all = local_call(
        functools.partial(pair_elements, steps, width),
        [(steps,) + square_shape, (steps, width, states), (steps,) + mean_shape, square_shape],
        psi,
        covar,
        mean,
        psi_other,
        covar_other,
        mean_other,
    )
    def over_core(blocks):
        return list(blocks) + [swapped(b, "col", 1) for b in blocks]

    while more:
        more = 4 * bit < n_seg
        came, psi_all, psi = lax.optimization_barrier((came, psi_all, psi))
        came = over_core(came)
        (total,) = local_call(
            functools.partial(joined_covariance, bit),
            [share_shape],
            psi_all,
            total,
            *came,
            scratch=[share_shape, share_shape, square_shape],
        )
        came_next = handed_up(total, 2 * bit)
        covar, mean = local_call(
            functools.partial(entered, bit),
            [(steps, width, states), (steps,) + mean_shape],
            psi,
            covar,
            mean,
            *came,
            scratch=[share_shape, share_shape, square_shape],
        )
        if more:
            step = over_core(step)
            (psi,) = local_call(
                functools.partial(matrices_entered, bit),
                [(steps,) + square_shape],
                psi,
                *step,
                scratch=[half_shape, half_shape],
            )
            (psi_all,) = local_call(
                functools.partial(joined_matrix, bit), [square_shape], psi_all, *step, scratch=[half_shape, half_shape]
            )
            psi_half = lax.dynamic_slice_in_dim(psi_all, col % 2 * (states // 2), states // 2, 0)
            step = handed_up(psi_half, 2 * bit, 1)
        came = came_next
        bit *= 2
    came, covar, step = lax.optimization_barrier((came, covar, step))
    covars, means = local_call(
        functools.partial(finished, bit, len(step)),
        [(steps, width, states), (steps, states)],
        psi,
        covar,
        mean,
        *over_core(step),
        *over_core(came),
        scratch=[share_shape, share_shape, square_shape, half_shape, half_shape]
        + [(steps * width, states), (steps * width + MEAN_ROWS, states)],
    )
    return means, covars


def solution(mesh):
    in_specs = (
        P("seg", "col", None),
        P("seg", None),
        P("seg", None),
        P("seg", None),
        P("seg", None),
        P(),
        P(),
        P("col", None),
        P(),
        P(),
    )
    out_specs = (P("seg", None), P("seg", "col", None))
    return jax.shard_map(
        per_device, mesh=mesh, in_specs=in_specs, out_specs=out_specs, check_vma=False
    )
```

```python
import functools

import jax
import jax.numpy as jnp
from jax import lax
from jax.experimental import pallas as pl
from jax.experimental.pallas import tpu as pltpu
from jax.sharding import PartitionSpec as P

F32, BF16 = jnp.float32, jnp.bfloat16
NN = (((1,), (0,)), ((), ()))
NT = (((1,), (1,)), ((), ()))
MEAN_ROWS = 16
CHUNKS = 4
COST = 7 * 10**8


def parts(x):
    high = x.astype(BF16)
    return high, (x - high.astype(F32)).astype(BF16)


def as_left(x):
    high, low = parts(x)
    return jnp.concatenate([high, high, low], axis=1)


def as_right(x, axis):
    high, low = parts(x)
    return jnp.concatenate([high, low, high], axis=axis)


def dot_nn(left, right):
    return lax.dot_general(as_left(left), as_right(right, 0), NN, preferred_element_type=F32)


def dot_nt(left, right):
    return lax.dot_general(as_left(left), as_right(right, 1), NT, preferred_element_type=F32)


def square(step, covar, mean):
    rows = covar.shape[0]
    both = dot_nt(jnp.concatenate([dot_nn(step, covar), mean], axis=0), step)
    return both[:rows], both[rows:]


def mean_block(row, states):
    return jnp.broadcast_to(row, (MEAN_ROWS, states))


def local_call(body, outs, *operands, scratch=(), copied=False, cost=0):
    shapes = [jax.ShapeDtypeStruct(shape, F32) for shape in outs]
    return pl.pallas_call(
        body,
        out_shape=shapes,
        name=getattr(body, "func", body).__name__,
        in_specs=[pl.BlockSpec(memory_space=pltpu.HBM if copied else pltpu.VMEM)] * len(operands),
        scratch_shapes=[pltpu.VMEM(o.shape, F32) for o in operands if copied]
        + [pltpu.SemaphoreType.DMA((len(operands) + CHUNKS,))] * copied
        + [pltpu.VMEM(shape, F32) for shape in scratch],
        compiler_params=pltpu.CompilerParams(vmem_limit_bytes=(58 if copied else 36) * 2**20),
        cost_estimate=pl.CostEstimate(
            flops=cost * COST, bytes_accessed=4096, transcendentals=0
        ),
    )(*operands)


def by_gain(left, right):
    return lax.dot_general(as_left(left), right, NT, preferred_element_type=F32)


def correction_rows(
    gain_hbm, oper_hbm, seen_hbm, keep_hbm, push_hbm, var_hbm, corr_ref, vec_ref,
    gain_ref, oper_ref, seen_ref, keep_ref, push_ref, var_ref, sems,
):
    width, states = corr_ref.shape
    steps = keep_ref.shape[0]
    observed = gain_hbm.shape[1]
    chunk = observed // CHUNKS
    pairs = [
        (oper_hbm, oper_ref),
        (seen_hbm, seen_ref),
        (keep_hbm, keep_ref),
        (push_hbm, push_ref),
        (var_hbm, var_ref),
    ]
    small = [pltpu.make_async_copy(a, b, sems.at[i]) for i, (a, b) in enumerate(pairs)]
    large = []
    for i in range(CHUNKS):
        at = pl.ds(i * chunk, chunk)
        large.append(pltpu.make_async_copy(gain_hbm.at[:, at], gain_ref.at[:, at], sems.at[len(pairs) + i]))
    for move in small[:2] + large + small[2:]:
        move.start()
    rows = lax.broadcasted_iota(jnp.int32, (width, states), 0) + lax.axis_index("col") * width
    cols = lax.broadcasted_iota(jnp.int32, (width, states), 1)
    small[0].wait()
    small[1].wait()
    blank = jnp.zeros((MEAN_ROWS - steps, observed), F32)
    left = jnp.concatenate([oper_ref[...], seen_ref[...], blank], axis=0)
    both = None
    for i in range(CHUNKS):
        at = slice(i * chunk, (i + 1) * chunk)
        large[i].wait()
        part = dot_nt(left[:, at], gain_ref[:, at])
        both = part if both is None else both + part
    corr_ref[...] = (rows == cols).astype(F32) - both[:width]
    for move in small[2:]:
        move.wait()
    for k in range(steps):
        here = slice(k, k + 1)
        vec_ref[k, 0:1, :] = keep_ref[here, :]
        vec_ref[k, 1:2, :] = var_ref[here, :]
        vec_ref[k, 2:3, :] = push_ref[here, :]
        vec_ref[k, 3:4, :] = both[width + k : width + k + 1]


def fixed_parts(gain_ref, noise_ref, factor_ref, fixed_ref, prior_ref):
    gain = gain_ref[...]
    fixed_ref[...] = by_gain(gain * noise_ref[...], as_right(gain, 1))

    @pl.when(lax.axis_index("seg") < 2)
    def _():
        prior_ref[...] = dot_nt(factor_ref[...], factor_ref[...])


def place(pieces, offsets, out_ref, base):
    me = lax.axis_index("col")
    width = pieces[0].shape[-2]
    for piece, offset in zip(pieces, offsets):
        at = pl.multiple_of((me ^ offset) * width + base, 8)
        out_ref[pl.ds(at, width), :] = piece


def noises(vec_ref, fixed_ref, corr_ref, noise_ref, offset_ref):
    steps, states = vec_ref.shape[0], corr_ref.shape[0]
    corr = corr_ref[...]
    vectors = [vec_ref[k] for k in range(steps)]
    push = [v[2:3] for v in vectors] + [jnp.zeros((MEAN_ROWS - steps, states), F32)]
    left = jnp.concatenate([corr * v[1:2] for v in vectors] + push, axis=0)
    both = dot_nt(left, corr)
    base = steps * states
    for k in range(steps):
        noise_ref[k] = both[k * states : (k + 1) * states] + fixed_ref[...]
        offset_ref[k] = mean_block(both[base + k : base + k + 1] + vectors[k][3:4], states)


def mixed_rows(out_ref, pieces, corr):
    steps, width = pieces[0].shape[:2]
    rows = jnp.concatenate([piece[k] for k in range(steps) for piece in pieces], axis=0)
    mixed = dot_nt(rows, corr)
    half = width * len(pieces)
    for k in range(steps):
        out_ref[k] = mixed[k * half : (k + 1) * half]


def own_rows(offsets, *refs):
    n_piece = len(offsets)
    pieces, own, (corr_ref, out_ref, work_ref) = refs[:n_piece], refs[n_piece:-3], refs[-3:]
    place([p[...] for p in pieces], offsets, work_ref, 0)
    corr_ref[...] = work_ref[...].T
    mixed_rows(out_ref, own, corr_ref[...])


def other_rows(corr_ref, *refs):
    mixed_rows(refs[-1], refs[:-1], corr_ref[...])


def matrices_of(offsets, vec_ref, corr, mine_ref, mate_ref, work_ref, out_ref):
    steps, half, states = mine_ref.shape
    width = half // len(offsets)
    for k in range(steps):
        for ref, bit in ((mine_ref, 0), (mate_ref, 1)):
            blocks = [ref[k, i * width : (i + 1) * width, :] for i in range(len(offsets))]
            place(blocks, [o ^ bit for o in offsets], work_ref, 0)
        out_ref[k] = work_ref[...].T + corr * vec_ref[k, 0:1, :]


def add_prior(step_ref, prior_ref, start_ref, covar_ref, mean_ref):
    covar, mean = square(step_ref[0], prior_ref[...], mean_block(start_ref[...], prior_ref.shape[0]))
    covar_ref[...] += covar
    mean_ref[...] += mean


def own_segment(
    offsets, vec_ref, corr_ref, mine_ref, mate_ref, noise_ref, offset_ref, prior_ref, start_ref,
    matrix_ref, psi_ref, covar_ref, mean_ref, work_ref,
):
    steps = matrix_ref.shape[0]
    matrices_of(offsets, vec_ref, corr_ref[...], mine_ref, mate_ref, work_ref, matrix_ref)
    covar_ref[0] = noise_ref[0]
    mean_ref[0] = offset_ref[0]

    @pl.when(lax.axis_index("seg") == 0)
    def _():
        add_prior(matrix_ref, prior_ref, start_ref, covar_ref.at[0], mean_ref.at[0])

    psi_ref[0] = matrix_ref[0]
    for k in range(1, steps):
        psi_ref[k] = dot_nn(matrix_ref[k], psi_ref[k - 1])
        covar, mean = square(matrix_ref[k], covar_ref[k - 1], mean_ref[k - 1])
        covar_ref[k] = covar + noise_ref[k]
        mean_ref[k] = mean + offset_ref[k]


def other_matrices(
    offsets, vec_ref, corr_ref, mine_ref, mate_ref, psi_ref, prior_ref, start_ref,
    matrix_ref, psi_other_ref, psi_half_ref, covar_ref, mean_ref, work_ref,
):
    steps, half, states = mine_ref.shape
    seg = lax.axis_index("seg")
    is_second = lax.rem(seg, 2) == 1
    matrices_of(offsets, vec_ref, corr_ref[...], mine_ref, mate_ref, work_ref, matrix_ref)
    mine = pl.ds(pl.multiple_of(lax.rem(lax.axis_index("col"), 2) * half, 8), half)
    covar_ref[...] = jnp.zeros_like(covar_ref)
    mean_ref[...] = jnp.zeros_like(mean_ref)

    @pl.when(seg == 1)
    def _():
        add_prior(matrix_ref, prior_ref, start_ref, covar_ref, mean_ref)

    @pl.when(seg < 2)
    def _():
        psi_half_ref[...] = jnp.zeros_like(psi_half_ref)

    @pl.when(seg >= 2)
    def _():
        psi_other_ref[...] = matrix_ref[0]
        for k in range(1, steps):
            psi_other_ref[...] = dot_nn(matrix_ref[k], psi_other_ref[...])

        @pl.when(is_second)
        def _():
            psi_half_ref[...] = dot_nn(psi_ref[steps - 1, mine, :], psi_other_ref[...])

        @pl.when(jnp.logical_not(is_second))
        def _():
            psi_half_ref[...] = dot_nn(psi_other_ref[mine, :], psi_ref[steps - 1])


def share_rows(edge):
    return 2 * edge + edge * 3 // 8 + 8


def masks(edge):
    rows = lax.broadcasted_iota(jnp.int32, (edge, edge), 0)
    cols = lax.broadcasted_iota(jnp.int32, (edge, edge), 1)
    return rows > cols, rows == cols


def put_packed(step_ref, covar, mean, added, out_ref):
    states = covar.shape[0]
    edge = states // 3
    half, part = edge // 2, edge * 3 // 8
    core = lax.rem(lax.axis_index("col"), 2)
    whole = added if callable(added) else lambda rows, cols: 0.0
    share = (lambda rows: 0.0) if callable(added) else (lambda rows: added[rows, :])

    def put(start, block):
        rows = slice(start, start + block.shape[0])
        out_ref[rows, :] = block + share(rows)
        return rows.stop

    @pl.when(core == 0)
    def _():
        rows = step_ref[: 2 * edge + part, :]
        low = dot_nt(dot_nn(rows, covar), rows[: 2 * edge])
        first, second = slice(0, edge), slice(edge, 2 * edge)
        last = slice(2 * edge, 2 * edge + part)
        below, on = masks(edge)
        corner = low[edge : 2 * edge, edge:] + whole(second, second)
        at = put(0, low[edge : 2 * edge, :edge] + whole(second, first))
        at = put(at, jnp.where(below | on, low[:edge, :edge] + whole(first, first), corner))
        at = put(at, low[2 * edge :, :edge] + whole(last, first))
        at = put(at, jnp.broadcast_to(jnp.sum(jnp.where(on, corner, 0.0), axis=0, keepdims=True), (8, edge)))

    @pl.when(core == 1)
    def _():
        rows = step_ref[2 * edge :, :]
        both = dot_nt(jnp.concatenate([dot_nn(rows, covar), mean], axis=0), step_ref[...])
        last, low = slice(2 * edge, states), both[:edge]
        row = both[edge : edge + 1]
        if callable(added):
            low = low + added(last, slice(0, states))
            row = row + added(None, slice(0, states))
        corner = low[:, 2 * edge :]
        at = put(0, low[part:, :edge])
        at = put(at, low[:, edge : 2 * edge])
        at = put(at, corner[half:])
        at = put(at, jnp.concatenate([corner[: half // 2, :half], corner[half // 2 : half, :half]], axis=1))
        rows = [row[:, j * edge : (j + 1) * edge] for j in range(3)]
        put(at, jnp.concatenate(rows + [jnp.zeros((5, edge), F32)], axis=0))


def unpacked(mine_ref, mate_ref, covar_ref):
    states = covar_ref.shape[0]
    edge = states // 3
    half, part = edge // 2, edge * 3 // 8
    is_low = lax.rem(lax.axis_index("col"), 2) == 0
    low = jnp.where(is_low, mine_ref[...], mate_ref[...])
    high = jnp.where(is_low, mate_ref[...], mine_ref[...])
    below, on = masks(edge)

    def put(i, j, block):
        covar_ref[i * edge : (i + 1) * edge, j * edge : (j + 1) * edge] = block
        if i != j:
            covar_ref[j * edge : (j + 1) * edge, i * edge : (i + 1) * edge] = block.T

    put(1, 0, low[:edge])
    mixed = low[edge : 2 * edge]
    turned = mixed.T
    put(0, 0, jnp.where(below | on, mixed, turned))
    diagonal = low[2 * edge + part : 2 * edge + part + 1]
    put(1, 1, jnp.where(on, diagonal, jnp.where(below, turned, mixed)))
    at = edge - part
    put(2, 0, jnp.concatenate([low[2 * edge : 2 * edge + part], high[:at]], axis=0))
    put(2, 1, high[at : at + edge])
    at += edge
    bottom = high[at : at + half]
    at += half
    folded = high[at : at + half // 2]
    at += half // 2
    quarter = jnp.concatenate([folded[:, :half], folded[:, half:]], axis=0)
    top = jnp.concatenate([quarter, bottom[:, :half].T], axis=1)
    put(2, 2, jnp.concatenate([top, bottom], axis=0))
    row = jnp.concatenate([high[at + j : at + j + 1] for j in range(3)], axis=1)
    return mean_block(row, states)


def pair_covariance(
    steps, psi_ref, covar_ref, mean_ref, noise_other_ref, offset_other_ref, matrix_other_ref, first_other_ref,
    first_mean_other_ref, covar_other_ref, mean_other_ref, out_ref, step_ref,
):
    states = first_other_ref.shape[0]
    edge = states // 3
    is_second = lax.rem(lax.axis_index("seg"), 2) == 1
    last = steps - 1

    @pl.when(is_second)
    def _():
        covar_other_ref[...] = noise_other_ref[0] + first_other_ref[...]
        mean_other_ref[...] = offset_other_ref[0] + first_mean_other_ref[...]
        step_ref[...] = psi_ref[last]

    @pl.when(jnp.logical_not(is_second))
    def _():
        covar_other_ref[...] = covar_ref[last]
        mean_other_ref[...] = mean_ref[last]
        step_ref[...] = matrix_other_ref[last]

    for k in range(last):
        at = k + is_second.astype(jnp.int32)
        covar, mean = square(matrix_other_ref[at], covar_other_ref[...], mean_other_ref[...])
        covar_other_ref[...] = covar + noise_other_ref[at]
        mean_other_ref[...] = mean + offset_other_ref[at]

    def added(rows, cols):
        if rows is None:
            return jnp.where(is_second, mean_ref[last, :1, cols], offset_other_ref[last, :1, cols])
        return jnp.where(is_second, covar_ref[last, rows, cols], noise_other_ref[last, rows, cols])

    put_packed(step_ref, covar_other_ref[...], mean_other_ref[...], added, out_ref)


def pair_elements(steps, width, psi_ref, covar_ref, mean_ref, psi_other_ref, covar_other_ref, mean_other_ref, *refs):
    psi_out_ref, covar_out_ref, mean_out_ref, psi_all_ref = refs
    seg = lax.axis_index("seg")
    is_second = lax.rem(seg, 2) == 1
    mine = pl.ds(pl.multiple_of(lax.axis_index("col") * width, 8), width)

    @pl.when(seg < 2)
    def _():
        psi_out_ref[...] = jnp.zeros_like(psi_out_ref)
        psi_all_ref[...] = jnp.zeros_like(psi_all_ref)

    @pl.when(seg >= 2)
    def _():
        for k in range(steps):

            @pl.when(is_second)
            def _():
                psi_out_ref[k] = dot_nn(psi_ref[k], psi_other_ref[...])

            @pl.when(jnp.logical_not(is_second))
            def _():
                psi_out_ref[k] = psi_ref[k]

        @pl.when(is_second)
        def _():
            psi_all_ref[...] = psi_out_ref[steps - 1]

        @pl.when(jnp.logical_not(is_second))
        def _():
            psi_all_ref[...] = dot_nn(psi_other_ref[...], psi_ref[steps - 1])

    @pl.when(is_second)
    def _():
        covar, mean = covar_other_ref[...], mean_other_ref[...]
        for k in range(steps):
            half = dot_nn(psi_ref[k, mine, :], covar)
            both = dot_nt(jnp.concatenate([half, mean], axis=0), psi_ref[k])
            covar_out_ref[k] = both[:width] + covar_ref[k, mine, :]
            mean_out_ref[k] = both[width:] + mean_ref[k]

    @pl.when(jnp.logical_not(is_second))
    def _():
        for k in range(steps):
            covar_out_ref[k] = covar_ref[k, mine, :]
            mean_out_ref[k] = mean_ref[k]


def whole_matrix(mine, mate):
    is_low = lax.rem(lax.axis_index("col"), 2) == 0
    return jnp.concatenate([jnp.where(is_low, mine, mate), jnp.where(is_low, mate, mine)], axis=0)


def place_in(bit):
    return lax.div(lax.rem(lax.axis_index("seg"), 2 * bit) - bit, 2) - (lax.rem(lax.axis_index("seg"), 2 * bit) < bit)


def is_upper(bit):
    return lax.rem(lax.axis_index("seg"), 2 * bit) >= bit


def chosen(refs, bit):
    at = place_in(bit)
    value = refs[0][...]
    for i, ref in enumerate(refs[1:]):
        value = jnp.where(at == i + 1, ref[...], value)
    return value


def joined_covariance(bit, psi_ref, total_ref, *refs):
    n_group = bit // 2
    mines, mates = refs[:n_group], refs[n_group : 2 * n_group]
    out_ref, mine_ref, mate_ref, work_ref = refs[2 * n_group :]

    at = lax.rem(lax.axis_index("seg"), 4 * bit)

    @pl.when((at >= 2 * bit - 2) & (at < 2 * bit))
    def _():
        mine_ref[...] = chosen(mines, bit)
        mate_ref[...] = chosen(mates, bit)
        mean = unpacked(mine_ref, mate_ref, work_ref)
        put_packed(psi_ref, work_ref[...], mean, total_ref, out_ref)


def chosen_matrix(refs, bit):
    n_group = bit // 2
    mine, *mate = [chosen(refs[i * n_group : (i + 1) * n_group], bit) for i in range(3)]
    return whole_matrix(mine, jnp.concatenate(mate, axis=0))


def joined_matrix(bit, psi_ref, *refs):
    refs[-1][...] = dot_nn(psi_ref[...], chosen_matrix(refs[:-1], bit))


def entered(bit, psi_ref, covar_ref, mean_ref, *refs):
    n_group = bit // 2
    mines, mates = refs[:n_group], refs[n_group : 2 * n_group]
    covar_out_ref, mean_out_ref, mine_ref, mate_ref, work_ref = refs[2 * n_group :]
    steps, width, states = covar_ref.shape
    mine = pl.ds(pl.multiple_of(lax.axis_index("col") * width, 8), width)

    @pl.when(is_upper(bit))
    def _():
        mine_ref[...] = chosen(mines, bit)
        mate_ref[...] = chosen(mates, bit)
        mean = unpacked(mine_ref, mate_ref, work_ref)
        covar = work_ref[...]
        for k in range(steps):
            half = dot_nn(psi_ref[k, mine, :], covar)
            both = dot_nt(jnp.concatenate([half, mean], axis=0), psi_ref[k])
            covar_out_ref[k] = both[:width] + covar_ref[k]
            mean_out_ref[k] = both[width:] + mean_ref[k]

    @pl.when(jnp.logical_not(is_upper(bit)))
    def _():
        covar_out_ref[...] = covar_ref[...]
        mean_out_ref[...] = mean_ref[...]


def takes_matrix(bit):
    return is_upper(bit) & (lax.axis_index("seg") >= 2 * bit)


def matrices_entered(bit, psi_ref, *refs):
    psi_out_ref = refs[-1]

    @pl.when(takes_matrix(bit))
    def _():
        before = chosen_matrix(refs[:-1], bit)
        for k in range(psi_ref.shape[0]):
            psi_out_ref[k] = dot_nn(psi_ref[k], before)

    @pl.when(jnp.logical_not(takes_matrix(bit)))
    def _():
        psi_out_ref[...] = psi_ref[...]


def finished(bit, psi_ref, covar_ref, mean_ref, *refs):
    n_group = bit // 2
    mines, mates = refs[:n_group], refs[n_group : 2 * n_group]
    covar_out_ref, mean_out_ref, mine_ref, mate_ref, work_ref = refs[2 * n_group :]
    steps, width, states = covar_ref.shape
    mine = pl.ds(pl.multiple_of(lax.axis_index("col") * width, 8), width)

    @pl.when(is_upper(bit))
    def _():
        mine_ref[...] = chosen(mines, bit)
        mate_ref[...] = chosen(mates, bit)
        mean = unpacked(mine_ref, mate_ref, work_ref)
        rows = jnp.concatenate([psi_ref[k, mine, :] for k in range(steps)], axis=0)
        half = dot_nn(rows, work_ref[...])
        for k in range(steps):
            part = half[k * width : (k + 1) * width]
            both = dot_nt(jnp.concatenate([part, mean], axis=0), psi_ref[k])
            covar_out_ref[k] = both[:width] + covar_ref[k]
            mean_out_ref[k : k + 1, :] = both[width : width + 1] + mean_ref[k, :1, :]

    @pl.when(jnp.logical_not(is_upper(bit)))
    def _():
        covar_out_ref[...] = covar_ref[...]
        for k in range(steps):
            mean_out_ref[k : k + 1, :] = mean_ref[k, :1, :]


def swapped(block, axis, bit):
    return lax.ppermute(block, axis, [(i, i ^ bit) for i in range(lax.axis_size(axis))])


def handed_up(block, bit, first=0):
    n_seg, n_col = lax.axis_size("seg"), lax.axis_size("col")
    came = []
    for group in range(bit // 2):
        aside = n_col // 2 if group % 2 == 0 else n_col
        to = {i: i ^ aside for i in range(n_seg * n_col)}
        for low in range(first * 2 * bit, n_seg, 2 * bit):
            for i in range((low + bit - 2) * n_col, (low + bit) * n_col):
                j = i + (2 + 2 * group) * n_col
                to[i], to[j] = j, i
        came.append(lax.ppermute(block, ("seg", "col"), sorted(to.items())))
    return came


def with_mate(share):
    return (share, swapped(share, "col", 1))


def per_device(
    model_mixing,
    retention,
    forcing,
    observations,
    model_noise,
    obs_noise,
    gain,
    obs_operator_t,
    prior_mean,
    prior_factor,
):
    steps, width, states = model_mixing.shape
    n_col, n_seg = lax.axis_size("col"), lax.axis_size("seg")
    col = lax.axis_index("col")
    edge = states // 3
    square_shape, mean_shape = (states, states), (MEAN_ROWS, states)
    share_shape, half_shape = (share_rows(edge), edge), (states // 2, states)
    far_bits = []
    bit = n_col // 2
    while bit > 1:
        far_bits.append(bit)
        bit //= 2
    offsets = [0]
    for bit in far_bits:
        offsets = offsets + [o ^ bit for o in offsets]

    own = [model_mixing]
    for bit in far_bits:
        own = own + [swapped(b, "col", bit) for b in own]
    near = swapped(model_mixing, "seg", 1)
    corr_mine, vectors = local_call(
        correction_rows,
        [(width, states), (steps, 4, states)],
        gain,
        obs_operator_t,
        observations,
        retention,
        forcing,
        model_noise,
        copied=True,
        cost=3,
    )
    corr_mine, gain = lax.optimization_barrier((corr_mine, gain))
    fixed, prior = local_call(
        fixed_parts, [square_shape, square_shape], gain, obs_noise[None, :], prior_factor
    )
    corr = [corr_mine]
    for bit in far_bits:
        corr = corr + [swapped(b, "col", bit) for b in corr]
    vectors_other = swapped(vectors, "seg", 1)
    own, near, fixed, vectors_other = lax.optimization_barrier((own, near, fixed, vectors_other))
    other = [near] + [swapped(b, "seg", 1) for b in own[1:]]
    corr = corr + [swapped(b, "col", 1) for b in corr]
    rows_shape = (steps,) + half_shape
    noise_shapes = [(steps,) + square_shape, (steps,) + mean_shape]
    correction, rows = local_call(
        functools.partial(own_rows, offsets + [o ^ 1 for o in offsets]),
        [square_shape, rows_shape],
        *corr,
        *own,
        scratch=[square_shape],
    )
    noise, offset = local_call(noises, noise_shapes, vectors, fixed, correction)
    start = prior_mean[None, :]
    noise_other, offset_other = local_call(noises, noise_shapes, vectors_other, fixed, correction)
    other, correction, noise, noise_other = lax.optimization_barrier((other, correction, noise, noise_other))
    (rows_other,) = local_call(other_rows, [rows_shape], correction, *other)
    matrix, psi, covar, mean = local_call(
        functools.partial(own_segment, offsets),
        [(steps,) + square_shape, (steps,) + square_shape, (steps,) + square_shape, (steps,) + mean_shape],
        vectors,
        correction,
        *with_mate(rows),
        noise,
        offset,
        prior,
        start,
        scratch=[square_shape],
        cost=1,
    )
    matrix_other, psi_other, psi_half, first_other, first_mean_other = local_call(
        functools.partial(other_matrices, offsets),
        [(steps,) + square_shape, square_shape, half_shape, square_shape, mean_shape],
        vectors_other,
        correction,
        *with_mate(rows_other),
        psi,
        prior,
        start,
        scratch=[square_shape],
    )
    bit = 2
    more = 2 * bit < n_seg
    covar_other, mean_other, total = local_call(
        functools.partial(pair_covariance, steps),
        [square_shape, mean_shape, share_shape],
        psi,
        covar,
        mean,
        noise_other,
        offset_other,
        matrix_other,
        first_other,
        first_mean_other,
        scratch=[square_shape],
    )
    total, psi_half = lax.optimization_barrier((total, psi_half))
    came = handed_up(total, bit)
    step = []
    if more:
        step = handed_up(psi_half, bit, 1)
    psi, covar, mean, psi_all = local_call(
        functools.partial(pair_elements, steps, width),
        [(steps,) + square_shape, (steps, width, states), (steps,) + mean_shape, square_shape],
        psi,
        covar,
        mean,
        psi_other,
        covar_other,
        mean_other,
    )
    def over_core(blocks):
        return list(blocks) + [swapped(b, "col", 1) for b in blocks]

    while more:
        more = 4 * bit < n_seg
        came, psi_all, psi = lax.optimization_barrier((came, psi_all, psi))
        came = over_core(came)
        (total,) = local_call(
            functools.partial(joined_covariance, bit),
            [share_shape],
            psi_all,
            total,
            *came,
            scratch=[share_shape, share_shape, square_shape],
        )
        came_next = handed_up(total, 2 * bit)
        covar, total = lax.optimization_barrier((covar, total))
        covar, mean = local_call(
            functools.partial(entered, bit),
            [(steps, width, states), (steps,) + mean_shape],
            psi,
            covar,
            mean,
            *came,
            scratch=[share_shape, share_shape, square_shape],
        )
        step, covar = lax.optimization_barrier((step, covar))
        for part in (slice(0, states // 4), slice(states // 4, states // 2)):
            step = step + [swapped(b[part], "col", 1) for b in step[: bit // 2]]
        if more:
            (psi_all,) = local_call(functools.partial(joined_matrix, bit), [square_shape], psi_all, *step)
            psi_half = lax.dynamic_slice_in_dim(psi_all, col % 2 * (states // 2), states // 2, 0)
        (psi,) = local_call(
            functools.partial(matrices_entered, bit), [(steps,) + square_shape], psi, *step
        )
        if more:
            step = handed_up(psi_half, 2 * bit, 1)
        came = came_next
        bit *= 2
    came, covar, psi = lax.optimization_barrier((came, covar, psi))
    covars, means = local_call(
        functools.partial(finished, bit),
        [(steps, width, states), (steps, states)],
        psi,
        covar,
        mean,
        *over_core(came),
        scratch=[share_shape, share_shape, square_shape],
    )
    return means, covars


def solution(mesh):
    in_specs = (
        P("seg", "col", None),
        P("seg", None),
        P("seg", None),
        P("seg", None),
        P("seg", None),
        P(),
        P(),
        P("col", None),
        P(),
        P(),
    )
    out_specs = (P("seg", None), P("seg", "col", None))
    return jax.shard_map(
        per_device, mesh=mesh, in_specs=in_specs, out_specs=out_specs, check_vma=False
    )
```

```python
import functools

import jax
import jax.numpy as jnp
from jax import lax
from jax.experimental import pallas as pl
from jax.experimental.pallas import tpu as pltpu
from jax.sharding import PartitionSpec as P

F32, BF16 = jnp.float32, jnp.bfloat16
NN = (((1,), (0,)), ((), ()))
NT = (((1,), (1,)), ((), ()))
MEAN_ROWS = 16
CHUNKS = 4
COST = 7 * 10**8


def parts(x):
    high = x.astype(BF16)
    return high, (x - high.astype(F32)).astype(BF16)


def as_left(x):
    high, low = parts(x)
    return jnp.concatenate([high, high, low], axis=1)


def as_right(x, axis):
    high, low = parts(x)
    return jnp.concatenate([high, low, high], axis=axis)


def dot_nn(left, right):
    return lax.dot_general(as_left(left), as_right(right, 0), NN, preferred_element_type=F32)


def dot_nt(left, right):
    return lax.dot_general(as_left(left), as_right(right, 1), NT, preferred_element_type=F32)


def square(step, covar, mean):
    rows = covar.shape[0]
    both = dot_nt(jnp.concatenate([dot_nn(step, covar), mean], axis=0), step)
    return both[:rows], both[rows:]


def mean_block(row, states):
    return jnp.broadcast_to(row, (MEAN_ROWS, states))


def local_call(body, outs, *operands, scratch=(), copied=False, cost=0):
    shapes = [jax.ShapeDtypeStruct(shape, F32) for shape in outs]
    return pl.pallas_call(
        body,
        out_shape=shapes,
        name=getattr(body, "func", body).__name__,
        in_specs=[pl.BlockSpec(memory_space=pltpu.HBM if copied else pltpu.VMEM)] * len(operands),
        scratch_shapes=[pltpu.VMEM(o.shape, F32) for o in operands if copied]
        + [pltpu.SemaphoreType.DMA((len(operands) + CHUNKS,))] * copied
        + [pltpu.VMEM(shape, F32) for shape in scratch],
        compiler_params=pltpu.CompilerParams(vmem_limit_bytes=(58 if copied else 36) * 2**20),
        cost_estimate=pl.CostEstimate(
            flops=cost * COST, bytes_accessed=4096, transcendentals=0
        ),
    )(*operands)


def by_gain(left, right):
    return lax.dot_general(as_left(left), right, NT, preferred_element_type=F32)


def correction_rows(
    gain_hbm, oper_hbm, seen_hbm, keep_hbm, push_hbm, var_hbm, corr_ref, vec_ref,
    gain_ref, oper_ref, seen_ref, keep_ref, push_ref, var_ref, sems,
):
    width, states = corr_ref.shape
    steps = keep_ref.shape[0]
    observed = gain_hbm.shape[1]
    chunk = observed // CHUNKS
    pairs = [
        (oper_hbm, oper_ref),
        (seen_hbm, seen_ref),
        (keep_hbm, keep_ref),
        (push_hbm, push_ref),
        (var_hbm, var_ref),
    ]
    small = [pltpu.make_async_copy(a, b, sems.at[i]) for i, (a, b) in enumerate(pairs)]
    large = []
    for i in range(CHUNKS):
        at = pl.ds(i * chunk, chunk)
        large.append(pltpu.make_async_copy(gain_hbm.at[:, at], gain_ref.at[:, at], sems.at[len(pairs) + i]))
    for move in small[:2] + large + small[2:]:
        move.start()
    rows = lax.broadcasted_iota(jnp.int32, (width, states), 0) + lax.axis_index("col") * width
    cols = lax.broadcasted_iota(jnp.int32, (width, states), 1)
    small[0].wait()
    small[1].wait()
    blank = jnp.zeros((MEAN_ROWS - steps, observed), F32)
    left = jnp.concatenate([oper_ref[...], seen_ref[...], blank], axis=0)
    both = None
    for i in range(CHUNKS):
        at = slice(i * chunk, (i + 1) * chunk)
        large[i].wait()
        part = dot_nt(left[:, at], gain_ref[:, at])
        both = part if both is None else both + part
    corr_ref[...] = (rows == cols).astype(F32) - both[:width]
    for move in small[2:]:
        move.wait()
    for k in range(steps):
        here = slice(k, k + 1)
        vec_ref[k, 0:1, :] = keep_ref[here, :]
        vec_ref[k, 1:2, :] = var_ref[here, :]
        vec_ref[k, 2:3, :] = push_ref[here, :]
        vec_ref[k, 3:4, :] = both[width + k : width + k + 1]


def fixed_parts(gain_ref, noise_ref, factor_ref, fixed_ref, prior_ref):
    gain = gain_ref[...]
    fixed_ref[...] = by_gain(gain * noise_ref[...], as_right(gain, 1))

    @pl.when(lax.axis_index("seg") < 2)
    def _():
        prior_ref[...] = dot_nt(factor_ref[...], factor_ref[...])


def place(pieces, offsets, out_ref, base):
    me = lax.axis_index("col")
    width = pieces[0].shape[-2]
    for piece, offset in zip(pieces, offsets):
        at = pl.multiple_of((me ^ offset) * width + base, 8)
        out_ref[pl.ds(at, width), :] = piece


def noises(vec_ref, push_ref, fixed_ref, corr_ref, noise_ref, offset_ref):
    steps, states = vec_ref.shape[0], corr_ref.shape[0]
    corr = corr_ref[...]
    right = jnp.concatenate([corr * vec_ref[k, 1:2, :] for k in range(steps)], axis=0)
    both = dot_nt(corr, right)
    for k in range(steps):
        noise_ref[k] = both[:, k * states : (k + 1) * states] + fixed_ref[...]
        offset_ref[k] = mean_block(push_ref[k : k + 1, :] + vec_ref[k, 3:4, :], states)


def mixed_rows(out_ref, pieces, corr, more=()):
    steps, width = pieces[0].shape[:2]
    rows = [piece[k] for k in range(steps) for piece in pieces] + list(more)
    mixed = dot_nt(jnp.concatenate(rows, axis=0), corr)
    half = width * len(pieces)
    for k in range(steps):
        out_ref[k] = mixed[k * half : (k + 1) * half]
    return mixed[steps * half :]


def own_rows(offsets, vec_ref, vec_other_ref, *refs):
    n_piece = len(offsets)
    pieces, own, (corr_ref, out_ref, push_ref, push_other_ref, work_ref) = refs[:n_piece], refs[n_piece:-5], refs[-5:]
    place([p[...] for p in pieces], offsets, work_ref, 0)
    corr_ref[...] = work_ref[...].T
    steps, states = vec_ref.shape[0], corr_ref.shape[0]
    push = [ref[k, 2:3, :] for ref in (vec_ref, vec_other_ref) for k in range(steps)]
    pushed = mixed_rows(
        out_ref, own, corr_ref[...], push + [jnp.zeros((MEAN_ROWS - 2 * steps, states), F32)]
    )
    push_ref[...] = pushed[:steps]
    push_other_ref[...] = pushed[steps : 2 * steps]


def other_rows(corr_ref, *refs):
    mixed_rows(refs[-1], refs[:-1], corr_ref[...])


def matrices_of(offsets, vec_ref, corr, mine_ref, mate_ref, work_ref, out_ref):
    steps, half, states = mine_ref.shape
    width = half // len(offsets)
    for k in range(steps):
        for ref, bit in ((mine_ref, 0), (mate_ref, 1)):
            blocks = [ref[k, i * width : (i + 1) * width, :] for i in range(len(offsets))]
            place(blocks, [o ^ bit for o in offsets], work_ref, 0)
        out_ref[k] = work_ref[...].T + corr * vec_ref[k, 0:1, :]


def add_prior(step_ref, prior_ref, start_ref, covar_ref, mean_ref):
    covar, mean = square(step_ref[0], prior_ref[...], mean_block(start_ref[...], prior_ref.shape[0]))
    covar_ref[...] += covar
    mean_ref[...] += mean


def own_segment(
    offsets, vec_ref, corr_ref, mine_ref, mate_ref, noise_ref, offset_ref, prior_ref, start_ref,
    matrix_ref, psi_ref, covar_ref, mean_ref, work_ref,
):
    steps = matrix_ref.shape[0]
    matrices_of(offsets, vec_ref, corr_ref[...], mine_ref, mate_ref, work_ref, matrix_ref)
    covar_ref[0] = noise_ref[0]
    mean_ref[0] = offset_ref[0]

    @pl.when(lax.axis_index("seg") == 0)
    def _():
        add_prior(matrix_ref, prior_ref, start_ref, covar_ref.at[0], mean_ref.at[0])

    psi_ref[0] = matrix_ref[0]
    for k in range(1, steps):

        @pl.when(lax.axis_index("seg") > 0)
        def _():
            psi_ref[k] = dot_nn(matrix_ref[k], psi_ref[k - 1])

        covar, mean = square(matrix_ref[k], covar_ref[k - 1], mean_ref[k - 1])
        covar_ref[k] = covar + noise_ref[k]
        mean_ref[k] = mean + offset_ref[k]


def other_matrices(
    offsets, vec_ref, corr_ref, mine_ref, mate_ref, prior_ref, start_ref, matrix_ref, covar_ref, mean_ref, work_ref
):
    matrices_of(offsets, vec_ref, corr_ref[...], mine_ref, mate_ref, work_ref, matrix_ref)
    covar_ref[...] = jnp.zeros_like(covar_ref)
    mean_ref[...] = jnp.zeros_like(mean_ref)

    @pl.when(lax.axis_index("seg") == 1)
    def _():
        add_prior(matrix_ref, prior_ref, start_ref, covar_ref, mean_ref)


def share_rows(edge):
    return 2 * edge + edge * 3 // 8 + 8


def masks(edge):
    rows = lax.broadcasted_iota(jnp.int32, (edge, edge), 0)
    cols = lax.broadcasted_iota(jnp.int32, (edge, edge), 1)
    return rows > cols, rows == cols


def put_packed(step_ref, covar, mean, added, out_ref):
    states = covar.shape[0]
    edge = states // 3
    half, part = edge // 2, edge * 3 // 8
    core = lax.rem(lax.axis_index("col"), 2)
    whole = added if callable(added) else lambda rows, cols: 0.0
    share = (lambda rows: 0.0) if callable(added) else (lambda rows: added[rows, :])

    def put(start, block):
        rows = slice(start, start + block.shape[0])
        out_ref[rows, :] = block + share(rows)
        return rows.stop

    @pl.when(core == 0)
    def _():
        rows = step_ref[: 2 * edge + part, :]
        low = dot_nt(dot_nn(rows, covar), rows[: 2 * edge])
        first, second = slice(0, edge), slice(edge, 2 * edge)
        last = slice(2 * edge, 2 * edge + part)
        below, on = masks(edge)
        corner = low[edge : 2 * edge, edge:] + whole(second, second)
        at = put(0, low[edge : 2 * edge, :edge] + whole(second, first))
        at = put(at, jnp.where(below | on, low[:edge, :edge] + whole(first, first), corner))
        at = put(at, low[2 * edge :, :edge] + whole(last, first))
        at = put(at, jnp.broadcast_to(jnp.sum(jnp.where(on, corner, 0.0), axis=0, keepdims=True), (8, edge)))

    @pl.when(core == 1)
    def _():
        rows = step_ref[2 * edge :, :]
        both = dot_nt(jnp.concatenate([dot_nn(rows, covar), mean], axis=0), step_ref[...])
        last, low = slice(2 * edge, states), both[:edge]
        row = both[edge : edge + 1]
        if callable(added):
            low = low + added(last, slice(0, states))
            row = row + added(None, slice(0, states))
        corner = low[:, 2 * edge :]
        at = put(0, low[part:, :edge])
        at = put(at, low[:, edge : 2 * edge])
        at = put(at, corner[half:])
        at = put(at, jnp.concatenate([corner[: half // 2, :half], corner[half // 2 : half, :half]], axis=1))
        rows = [row[:, j * edge : (j + 1) * edge] for j in range(3)]
        put(at, jnp.concatenate(rows + [jnp.zeros((5, edge), F32)], axis=0))


def unpacked(mine_ref, mate_ref, covar_ref):
    states = covar_ref.shape[0]
    edge = states // 3
    half, part = edge // 2, edge * 3 // 8
    is_low = lax.rem(lax.axis_index("col"), 2) == 0
    low = jnp.where(is_low, mine_ref[...], mate_ref[...])
    high = jnp.where(is_low, mate_ref[...], mine_ref[...])
    below, on = masks(edge)

    def put(i, j, block):
        covar_ref[i * edge : (i + 1) * edge, j * edge : (j + 1) * edge] = block
        if i != j:
            covar_ref[j * edge : (j + 1) * edge, i * edge : (i + 1) * edge] = block.T

    put(1, 0, low[:edge])
    mixed = low[edge : 2 * edge]
    turned = mixed.T
    put(0, 0, jnp.where(below | on, mixed, turned))
    diagonal = low[2 * edge + part : 2 * edge + part + 1]
    put(1, 1, jnp.where(on, diagonal, jnp.where(below, turned, mixed)))
    at = edge - part
    put(2, 0, jnp.concatenate([low[2 * edge : 2 * edge + part], high[:at]], axis=0))
    put(2, 1, high[at : at + edge])
    at += edge
    bottom = high[at : at + half]
    at += half
    folded = high[at : at + half // 2]
    at += half // 2
    quarter = jnp.concatenate([folded[:, :half], folded[:, half:]], axis=0)
    top = jnp.concatenate([quarter, bottom[:, :half].T], axis=1)
    put(2, 2, jnp.concatenate([top, bottom], axis=0))
    row = jnp.concatenate([high[at + j : at + j + 1] for j in range(3)], axis=1)
    return mean_block(row, states)


def pair_covariance(
    steps, psi_ref, covar_ref, mean_ref, noise_other_ref, offset_other_ref, matrix_other_ref, first_other_ref,
    first_mean_other_ref, covar_other_ref, mean_other_ref, out_ref, step_ref,
):
    states = first_other_ref.shape[0]
    edge = states // 3
    is_second = lax.rem(lax.axis_index("seg"), 2) == 1
    last = steps - 1

    @pl.when(is_second)
    def _():
        covar_other_ref[...] = noise_other_ref[0] + first_other_ref[...]
        mean_other_ref[...] = offset_other_ref[0] + first_mean_other_ref[...]
        step_ref[...] = psi_ref[last]

    @pl.when(jnp.logical_not(is_second))
    def _():
        covar_other_ref[...] = covar_ref[last]
        mean_other_ref[...] = mean_ref[last]
        step_ref[...] = matrix_other_ref[last]

    for k in range(last):
        at = k + is_second.astype(jnp.int32)
        covar, mean = square(matrix_other_ref[at], covar_other_ref[...], mean_other_ref[...])
        covar_other_ref[...] = covar + noise_other_ref[at]
        mean_other_ref[...] = mean + offset_other_ref[at]

    def added(rows, cols):
        if rows is None:
            return jnp.where(is_second, mean_ref[last, :1, cols], offset_other_ref[last, :1, cols])
        return jnp.where(is_second, covar_ref[last, rows, cols], noise_other_ref[last, rows, cols])

    put_packed(step_ref, covar_other_ref[...], mean_other_ref[...], added, out_ref)


def pair_matrices(matrix_ref, psi_ref, psi_other_ref, psi_all_ref, half_ref):
    steps, states = matrix_ref.shape[:2]
    half = states // 2
    seg = lax.axis_index("seg")
    mine = pl.ds(pl.multiple_of(lax.rem(lax.axis_index("col"), 2) * half, 8), half)

    @pl.when(seg < 2)
    def _():
        psi_other_ref[...] = jnp.zeros_like(psi_other_ref)
        psi_all_ref[...] = jnp.zeros_like(psi_all_ref)
        half_ref[...] = jnp.zeros_like(half_ref)

    @pl.when(seg >= 2)
    def _():
        psi_other_ref[...] = matrix_ref[0]
        for k in range(1, steps):
            psi_other_ref[...] = dot_nn(matrix_ref[k], psi_other_ref[...])
        own, other = psi_ref[steps - 1], psi_other_ref[...]
        is_second = lax.rem(seg, 2) == 1
        psi_all_ref[...] = dot_nn(jnp.where(is_second, own, other), jnp.where(is_second, other, own))
        half_ref[...] = psi_all_ref[mine, :]


def pair_elements(steps, width, psi_ref, covar_ref, mean_ref, psi_other_ref, psi_all_ref, covar_other_ref, mean_other_ref, *refs):
    psi_out_ref, covar_out_ref, mean_out_ref = refs
    seg = lax.axis_index("seg")
    is_second = lax.rem(seg, 2) == 1
    mine = pl.ds(pl.multiple_of(lax.axis_index("col") * width, 8), width)

    @pl.when(seg < 2)
    def _():
        psi_out_ref[...] = jnp.zeros_like(psi_out_ref)

    @pl.when((seg >= 2) & is_second)
    def _():
        for k in range(steps - 1):
            psi_out_ref[k] = dot_nn(psi_ref[k], psi_other_ref[...])
        psi_out_ref[steps - 1] = psi_all_ref[...]

    @pl.when((seg >= 2) & jnp.logical_not(is_second))
    def _():
        psi_out_ref[...] = psi_ref[...]

    @pl.when(is_second)
    def _():
        covar, mean = covar_other_ref[...], mean_other_ref[...]
        for k in range(steps):
            half = dot_nn(psi_ref[k, mine, :], covar)
            both = dot_nt(jnp.concatenate([half, mean], axis=0), psi_ref[k])
            covar_out_ref[k] = both[:width] + covar_ref[k, mine, :]
            mean_out_ref[k] = both[width:] + mean_ref[k]

    @pl.when(jnp.logical_not(is_second))
    def _():
        for k in range(steps):
            covar_out_ref[k] = covar_ref[k, mine, :]
            mean_out_ref[k] = mean_ref[k]


def whole_matrix(mine, mate):
    is_low = lax.rem(lax.axis_index("col"), 2) == 0
    return jnp.concatenate([jnp.where(is_low, mine, mate), jnp.where(is_low, mate, mine)], axis=0)


def place_in(bit):
    return lax.div(lax.rem(lax.axis_index("seg"), 2 * bit) - bit, 2) - (lax.rem(lax.axis_index("seg"), 2 * bit) < bit)


def is_upper(bit):
    return lax.rem(lax.axis_index("seg"), 2 * bit) >= bit


def chosen(refs, bit):
    at = place_in(bit)
    value = refs[0][...]
    for i, ref in enumerate(refs[1:]):
        value = jnp.where(at == i + 1, ref[...], value)
    return value


def joined_covariance(bit, psi_ref, total_ref, *refs):
    n_group = bit // 2
    mines, mates = refs[:n_group], refs[n_group : 2 * n_group]
    out_ref, mine_ref, mate_ref, work_ref = refs[2 * n_group :]

    seg, last = lax.axis_index("seg"), lax.axis_size("seg") - 2

    @pl.when((lax.rem(seg, 2 * bit) >= 2 * bit - 2) & (seg < last))
    def _():
        mine_ref[...] = chosen(mines, bit)
        mate_ref[...] = chosen(mates, bit)
        mean = unpacked(mine_ref, mate_ref, work_ref)
        put_packed(psi_ref, work_ref[...], mean, total_ref, out_ref)


def chosen_matrix(refs, bit):
    n_group = bit // 2
    mine, *mate = [chosen(refs[i * n_group : (i + 1) * n_group], bit) for i in range(3)]
    return whole_matrix(mine, jnp.concatenate(mate, axis=0))


def joined_matrix(bit, psi_ref, *refs):
    refs[-1][...] = dot_nn(psi_ref[...], chosen_matrix(refs[:-1], bit))


def entered(bit, psi_ref, covar_ref, mean_ref, *refs):
    n_group = bit // 2
    mines, mates = refs[:n_group], refs[n_group : 2 * n_group]
    covar_out_ref, mean_out_ref, mine_ref, mate_ref, work_ref = refs[2 * n_group :]
    steps, width, states = covar_ref.shape
    mine = pl.ds(pl.multiple_of(lax.axis_index("col") * width, 8), width)

    @pl.when(is_upper(bit))
    def _():
        mine_ref[...] = chosen(mines, bit)
        mate_ref[...] = chosen(mates, bit)
        mean = unpacked(mine_ref, mate_ref, work_ref)
        covar = work_ref[...]
        for k in range(steps):
            half = dot_nn(psi_ref[k, mine, :], covar)
            both = dot_nt(jnp.concatenate([half, mean], axis=0), psi_ref[k])
            covar_out_ref[k] = both[:width] + covar_ref[k]
            mean_out_ref[k] = both[width:] + mean_ref[k]

    @pl.when(jnp.logical_not(is_upper(bit)))
    def _():
        covar_out_ref[...] = covar_ref[...]
        mean_out_ref[...] = mean_ref[...]


def takes_matrix(bit):
    return is_upper(bit) & (lax.axis_index("seg") >= 2 * bit)


def matrices_entered(bit, psi_ref, *refs):
    psi_out_ref = refs[-1]

    @pl.when(takes_matrix(bit))
    def _():
        before = chosen_matrix(refs[:-1], bit)
        for k in range(psi_ref.shape[0]):
            psi_out_ref[k] = dot_nn(psi_ref[k], before)

    @pl.when(jnp.logical_not(takes_matrix(bit)))
    def _():
        psi_out_ref[...] = psi_ref[...]


def finished(bit, psi_ref, covar_ref, mean_ref, *refs):
    n_group = bit // 2
    mines, mates = refs[:n_group], refs[n_group : 2 * n_group]
    covar_out_ref, mean_out_ref, mine_ref, mate_ref, work_ref = refs[2 * n_group :]
    steps, width, states = covar_ref.shape
    mine = pl.ds(pl.multiple_of(lax.axis_index("col") * width, 8), width)

    @pl.when(is_upper(bit))
    def _():
        mine_ref[...] = chosen(mines, bit)
        mate_ref[...] = chosen(mates, bit)
        mean = unpacked(mine_ref, mate_ref, work_ref)
        rows = jnp.concatenate([psi_ref[k, mine, :] for k in range(steps)], axis=0)
        half = dot_nn(rows, work_ref[...])
        for k in range(steps):
            part = half[k * width : (k + 1) * width]
            both = dot_nt(jnp.concatenate([part, mean], axis=0), psi_ref[k])
            covar_out_ref[k] = both[:width] + covar_ref[k]
            mean_out_ref[k : k + 1, :] = both[width : width + 1] + mean_ref[k, :1, :]

    @pl.when(jnp.logical_not(is_upper(bit)))
    def _():
        covar_out_ref[...] = covar_ref[...]
        for k in range(steps):
            mean_out_ref[k : k + 1, :] = mean_ref[k, :1, :]


def swapped(block, axis, bit):
    return lax.ppermute(block, axis, [(i, i ^ bit) for i in range(lax.axis_size(axis))])


def handed_up(block, bit, first=0):
    n_seg, n_col = lax.axis_size("seg"), lax.axis_size("col")
    came = []
    for group in range(bit // 2):
        aside = n_col // 2 if group % 2 == 0 else n_col
        to = {i: i ^ aside for i in range(n_seg * n_col)}
        for low in range(first * 2 * bit, n_seg, 2 * bit):
            for i in range((low + bit - 2) * n_col, (low + bit) * n_col):
                j = i + (2 + 2 * group) * n_col
                to[i], to[j] = j, i
        came.append(lax.ppermute(block, ("seg", "col"), sorted(to.items())))
    return came


def with_mate(share):
    return (share, swapped(share, "col", 1))


def per_device(
    model_mixing,
    retention,
    forcing,
    observations,
    model_noise,
    obs_noise,
    gain,
    obs_operator_t,
    prior_mean,
    prior_factor,
):
    steps, width, states = model_mixing.shape
    n_col, n_seg = lax.axis_size("col"), lax.axis_size("seg")
    col = lax.axis_index("col")
    edge = states // 3
    square_shape, mean_shape = (states, states), (MEAN_ROWS, states)
    share_shape, half_shape = (share_rows(edge), edge), (states // 2, states)
    far_bits = []
    bit = n_col // 2
    while bit > 1:
        far_bits.append(bit)
        bit //= 2
    offsets = [0]
    for bit in far_bits:
        offsets = offsets + [o ^ bit for o in offsets]

    own = [model_mixing]
    for bit in far_bits:
        own = own + [swapped(b, "col", bit) for b in own]
    near = swapped(model_mixing, "seg", 1)
    corr_mine, vectors = local_call(
        correction_rows,
        [(width, states), (steps, 4, states)],
        gain,
        obs_operator_t,
        observations,
        retention,
        forcing,
        model_noise,
        copied=True,
        cost=3,
    )
    corr_mine, gain = lax.optimization_barrier((corr_mine, gain))
    fixed, prior = local_call(
        fixed_parts, [square_shape, square_shape], gain, obs_noise[None, :], prior_factor
    )
    corr = [corr_mine]
    for bit in far_bits:
        corr = corr + [swapped(b, "col", bit) for b in corr]
    vectors_other = swapped(vectors, "seg", 1)
    own, near, fixed, vectors_other = lax.optimization_barrier((own, near, fixed, vectors_other))
    other = [near] + [swapped(b, "seg", 1) for b in own[1:]]
    corr = corr + [swapped(b, "col", 1) for b in corr]
    rows_shape = (steps,) + half_shape
    noise_shapes = [(steps,) + square_shape, (steps,) + mean_shape]
    correction, rows, push, push_other = local_call(
        functools.partial(own_rows, offsets + [o ^ 1 for o in offsets]),
        [square_shape, rows_shape, (steps, states), (steps, states)],
        vectors,
        vectors_other,
        *corr,
        *own,
        scratch=[square_shape],
    )
    noise, offset = local_call(noises, noise_shapes, vectors, push, fixed, correction)
    start = prior_mean[None, :]
    noise_other, offset_other = local_call(
        noises, noise_shapes, vectors_other, push_other, fixed, correction
    )
    other, correction, noise, noise_other = lax.optimization_barrier((other, correction, noise, noise_other))
    (rows_other,) = local_call(other_rows, [rows_shape], correction, *other)
    matrix, psi, covar, mean = local_call(
        functools.partial(own_segment, offsets),
        [(steps,) + square_shape, (steps,) + square_shape, (steps,) + square_shape, (steps,) + mean_shape],
        vectors,
        correction,
        *with_mate(rows),
        noise,
        offset,
        prior,
        start,
        scratch=[square_shape],
        cost=1,
    )
    matrix_other, first_other, first_mean_other = local_call(
        functools.partial(other_matrices, offsets),
        [(steps,) + square_shape, square_shape, mean_shape],
        vectors_other,
        correction,
        *with_mate(rows_other),
        prior,
        start,
        scratch=[square_shape],
    )
    bit = 2
    more = 2 * bit < n_seg
    covar_other, mean_other, total = local_call(
        functools.partial(pair_covariance, steps),
        [square_shape, mean_shape, share_shape],
        psi,
        covar,
        mean,
        noise_other,
        offset_other,
        matrix_other,
        first_other,
        first_mean_other,
        scratch=[square_shape],
    )
    came = handed_up(total, bit)
    matrix_other, total = lax.optimization_barrier((matrix_other, total))
    psi_other, psi_all, psi_half = local_call(
        pair_matrices, [square_shape, square_shape, half_shape], matrix_other, psi
    )
    step = []
    if more:
        step = handed_up(psi_half, bit, 1)
    psi, covar, mean = local_call(
        functools.partial(pair_elements, steps, width),
        [(steps,) + square_shape, (steps, width, states), (steps,) + mean_shape],
        psi,
        covar,
        mean,
        psi_other,
        psi_all,
        covar_other,
        mean_other,
    )

    def over_core(blocks):
        return list(blocks) + [swapped(b, "col", 1) for b in blocks]

    while more:
        more = 4 * bit < n_seg
        came, psi_all, psi = lax.optimization_barrier((came, psi_all, psi))
        came = over_core(came)
        (total,) = local_call(
            functools.partial(joined_covariance, bit),
            [share_shape],
            psi_all,
            total,
            *came,
            scratch=[share_shape, share_shape, square_shape],
        )
        came_next = handed_up(total, 2 * bit)
        covar, total = lax.optimization_barrier((covar, total))
        covar, mean = local_call(
            functools.partial(entered, bit),
            [(steps, width, states), (steps,) + mean_shape],
            psi,
            covar,
            mean,
            *came,
            scratch=[share_shape, share_shape, square_shape],
        )
        step, covar = lax.optimization_barrier((step, covar))
        for part in (slice(0, states // 4), slice(states // 4, states // 2)):
            step = step + [swapped(b[part], "col", 1) for b in step[: bit // 2]]
        if more:
            (psi_all,) = local_call(functools.partial(joined_matrix, bit), [square_shape], psi_all, *step)
            psi_half = lax.dynamic_slice_in_dim(psi_all, col % 2 * (states // 2), states // 2, 0)
        (psi,) = local_call(
            functools.partial(matrices_entered, bit), [(steps,) + square_shape], psi, *step
        )
        if more:
            step = handed_up(psi_half, 2 * bit, 1)
        came = came_next
        bit *= 2
    came, covar, psi = lax.optimization_barrier((came, covar, psi))
    covars, means = local_call(
        functools.partial(finished, bit),
        [(steps, width, states), (steps, states)],
        psi,
        covar,
        mean,
        *over_core(came),
        scratch=[share_shape, share_shape, square_shape],
    )
    return means, covars


def solution(mesh):
    in_specs = (
        P("seg", "col", None),
        P("seg", None),
        P("seg", None),
        P("seg", None),
        P("seg", None),
        P(),
        P(),
        P("col", None),
        P(),
        P(),
    )
    out_specs = (P("seg", None), P("seg", "col", None))
    return jax.shard_map(
        per_device, mesh=mesh, in_specs=in_specs, out_specs=out_specs, check_vma=False
    )
```

```python
import functools

import jax
import jax.numpy as jnp
from jax import lax
from jax.experimental import pallas as pl
from jax.experimental.pallas import tpu as pltpu
from jax.sharding import PartitionSpec as P

F32, BF16 = jnp.float32, jnp.bfloat16
NN = (((1,), (0,)), ((), ()))
NT = (((1,), (1,)), ((), ()))
MEAN_ROWS = 16
CHUNKS = 4
COST = 7 * 10**8


def parts(x):
    high = x.astype(BF16)
    return high, (x - high.astype(F32)).astype(BF16)


def as_left(x):
    high, low = parts(x)
    return jnp.concatenate([high, high, low], axis=1)


def as_right(x, axis):
    high, low = parts(x)
    return jnp.concatenate([high, low, high], axis=axis)


def dot_nn(left, right):
    return lax.dot_general(as_left(left), as_right(right, 0), NN, preferred_element_type=F32)


def dot_nt(left, right):
    return lax.dot_general(as_left(left), as_right(right, 1), NT, preferred_element_type=F32)


def few_rows_dot(left, right, kind):
    rows = left.shape[0]
    left, right = parts(left), parts(right)
    both = lax.dot_general(jnp.concatenate(left, axis=0), right[0], kind, preferred_element_type=F32)
    return both[:rows] + (both[rows:] + lax.dot_general(left[0], right[1], kind, preferred_element_type=F32))


def stacked(left, right):
    return lax.dot_general(left, right, NT, preferred_element_type=F32)


def square(step, covar, mean):
    rows = covar.shape[0]
    edge = rows // 3
    half = dot_nn(step, covar)
    right = as_right(step, 1)
    top = stacked(as_left(half[: 2 * edge]), right[: 2 * edge])
    low = stacked(as_left(jnp.concatenate([half[2 * edge :], mean], axis=0)), right)
    block, last = top[edge:, :edge], low[:edge, : 2 * edge]
    first = jnp.concatenate([top[:edge, :edge], block.T, last[:, :edge].T], axis=1)
    second = jnp.concatenate([block, top[edge:, edge:], last[:, edge:].T], axis=1)
    return jnp.concatenate([first, second, low[:edge]], axis=0), low[edge:]


def mean_block(row, states):
    return jnp.broadcast_to(row, (MEAN_ROWS, states))


def local_call(body, outs, *operands, scratch=(), copied=False, cost=0):
    shapes = [jax.ShapeDtypeStruct(shape, F32) for shape in outs]
    return pl.pallas_call(
        body,
        out_shape=shapes,
        name=getattr(body, "func", body).__name__,
        in_specs=[pl.BlockSpec(memory_space=pltpu.HBM if copied else pltpu.VMEM)] * len(operands),
        scratch_shapes=[pltpu.VMEM(o.shape, F32) for o in operands if copied]
        + [pltpu.SemaphoreType.DMA((len(operands) + CHUNKS,))] * copied
        + [pltpu.VMEM(shape, F32) for shape in scratch],
        compiler_params=pltpu.CompilerParams(vmem_limit_bytes=(58 if copied else 36) * 2**20),
        cost_estimate=pl.CostEstimate(
            flops=cost * COST, bytes_accessed=4096, transcendentals=0
        ),
    )(*operands)


def by_gain(left, right):
    return lax.dot_general(as_left(left), right, NT, preferred_element_type=F32)


def correction_rows(
    gain_hbm, oper_hbm, seen_hbm, keep_hbm, push_hbm, var_hbm, corr_ref, vec_ref,
    gain_ref, oper_ref, seen_ref, keep_ref, push_ref, var_ref, sems,
):
    width, states = corr_ref.shape
    steps = keep_ref.shape[0]
    observed = gain_hbm.shape[1]
    chunk = observed // CHUNKS
    pairs = [
        (oper_hbm, oper_ref),
        (seen_hbm, seen_ref),
        (keep_hbm, keep_ref),
        (push_hbm, push_ref),
        (var_hbm, var_ref),
    ]
    small = [pltpu.make_async_copy(a, b, sems.at[i]) for i, (a, b) in enumerate(pairs)]
    large = []
    for i in range(CHUNKS):
        at = pl.ds(i * chunk, chunk)
        large.append(pltpu.make_async_copy(gain_hbm.at[:, at], gain_ref.at[:, at], sems.at[len(pairs) + i]))
    for move in small[:2] + large + small[2:]:
        move.start()
    rows = lax.broadcasted_iota(jnp.int32, (width, states), 0) + lax.axis_index("col") * width
    cols = lax.broadcasted_iota(jnp.int32, (width, states), 1)
    small[0].wait()
    small[1].wait()
    blank = jnp.zeros((MEAN_ROWS - steps, observed), F32)
    left = jnp.concatenate([oper_ref[...], seen_ref[...], blank], axis=0)
    both = None
    for i in range(CHUNKS):
        at = slice(i * chunk, (i + 1) * chunk)
        large[i].wait()
        part = dot_nt(left[:, at], gain_ref[:, at])
        both = part if both is None else both + part
    corr_ref[...] = (rows == cols).astype(F32) - both[:width]
    for move in small[2:]:
        move.wait()
    for k in range(steps):
        here = slice(k, k + 1)
        vec_ref[k, 0:1, :] = keep_ref[here, :]
        vec_ref[k, 1:2, :] = var_ref[here, :]
        vec_ref[k, 2:3, :] = push_ref[here, :]
        vec_ref[k, 3:4, :] = both[width + k : width + k + 1]


def fixed_parts(gain_ref, noise_ref, factor_ref, fixed_ref, prior_ref):
    gain = gain_ref[...]
    fixed_ref[...] = by_gain(gain * noise_ref[...], as_right(gain, 1))

    @pl.when(lax.axis_index("seg") < 2)
    def _():
        prior_ref[...] = dot_nt(factor_ref[...], factor_ref[...])


def place(pieces, offsets, out_ref, base):
    me = lax.axis_index("col")
    width = pieces[0].shape[-2]
    for piece, offset in zip(pieces, offsets):
        at = pl.multiple_of((me ^ offset) * width + base, 8)
        out_ref[pl.ds(at, width), :] = piece


def noises(vec_ref, push_ref, fixed_ref, corr_ref, noise_ref, offset_ref):
    steps, states = vec_ref.shape[0], corr_ref.shape[0]
    corr = corr_ref[...]
    right = jnp.concatenate([corr * vec_ref[k, 1:2, :] for k in range(steps)], axis=0)
    both = dot_nt(corr, right)
    for k in range(steps):
        noise_ref[k] = both[:, k * states : (k + 1) * states] + fixed_ref[...]
        offset_ref[k] = mean_block(push_ref[k : k + 1, :] + vec_ref[k, 3:4, :], states)


def mixed_rows(out_ref, pieces, corr, more=()):
    steps, width = pieces[0].shape[:2]
    rows = [piece[k] for k in range(steps) for piece in pieces] + list(more)
    mixed = dot_nt(jnp.concatenate(rows, axis=0), corr)
    half = width * len(pieces)
    for k in range(steps):
        out_ref[k] = mixed[k * half : (k + 1) * half]
    return mixed[steps * half :]


def own_rows(offsets, vec_ref, vec_other_ref, *refs):
    n_piece = len(offsets)
    pieces, own, (corr_ref, out_ref, push_ref, push_other_ref, work_ref) = refs[:n_piece], refs[n_piece:-5], refs[-5:]
    place([p[...] for p in pieces], offsets, work_ref, 0)
    corr_ref[...] = work_ref[...].T
    steps, states = vec_ref.shape[0], corr_ref.shape[0]
    push = [ref[k, 2:3, :] for ref in (vec_ref, vec_other_ref) for k in range(steps)]
    pushed = mixed_rows(
        out_ref, own, corr_ref[...], push + [jnp.zeros((MEAN_ROWS - 2 * steps, states), F32)]
    )
    push_ref[...] = pushed[:steps]
    push_other_ref[...] = pushed[steps : 2 * steps]


def other_rows(corr_ref, *refs):
    mixed_rows(refs[-1], refs[:-1], corr_ref[...])


def matrices_of(offsets, vec_ref, corr, mine_ref, mate_ref, work_ref, out_ref):
    steps, half, states = mine_ref.shape
    width = half // len(offsets)
    for k in range(steps):
        for ref, bit in ((mine_ref, 0), (mate_ref, 1)):
            blocks = [ref[k, i * width : (i + 1) * width, :] for i in range(len(offsets))]
            place(blocks, [o ^ bit for o in offsets], work_ref, 0)
        out_ref[k] = work_ref[...].T + corr * vec_ref[k, 0:1, :]


def add_prior(step_ref, prior_ref, start_ref, covar_ref, mean_ref):
    covar, mean = square(step_ref[0], prior_ref[...], mean_block(start_ref[...], prior_ref.shape[0]))
    covar_ref[...] += covar
    mean_ref[...] += mean


def own_segment(
    offsets, vec_ref, corr_ref, mine_ref, mate_ref, noise_ref, offset_ref, prior_ref, start_ref,
    matrix_ref, psi_ref, covar_ref, mean_ref, work_ref,
):
    steps = matrix_ref.shape[0]
    matrices_of(offsets, vec_ref, corr_ref[...], mine_ref, mate_ref, work_ref, matrix_ref)
    covar_ref[0] = noise_ref[0]
    mean_ref[0] = offset_ref[0]

    @pl.when(lax.axis_index("seg") == 0)
    def _():
        add_prior(matrix_ref, prior_ref, start_ref, covar_ref.at[0], mean_ref.at[0])

    psi_ref[0] = matrix_ref[0]
    for k in range(1, steps):

        @pl.when(lax.axis_index("seg") > 0)
        def _():
            psi_ref[k] = dot_nn(matrix_ref[k], psi_ref[k - 1])

        covar, mean = square(matrix_ref[k], covar_ref[k - 1], mean_ref[k - 1])
        covar_ref[k] = covar + noise_ref[k]
        mean_ref[k] = mean + offset_ref[k]


def share_rows(edge):
    return 2 * edge + edge * 3 // 8 + 8


def masks(edge):
    rows = lax.broadcasted_iota(jnp.int32, (edge, edge), 0)
    cols = lax.broadcasted_iota(jnp.int32, (edge, edge), 1)
    return rows > cols, rows == cols


def put_packed(step_ref, covar, mean, added, out_ref):
    states = covar.shape[0]
    edge = states // 3
    half, part = edge // 2, edge * 3 // 8
    core = lax.rem(lax.axis_index("col"), 2)
    whole = added if callable(added) else lambda rows, cols: 0.0
    share = (lambda rows: 0.0) if callable(added) else (lambda rows: added[rows, :])

    def put(start, block):
        rows = slice(start, start + block.shape[0])
        out_ref[rows, :] = block + share(rows)
        return rows.stop

    @pl.when(core == 0)
    def _():
        rows = step_ref[: 2 * edge + part, :]
        low = dot_nt(dot_nn(rows, covar), rows[: 2 * edge])
        first, second = slice(0, edge), slice(edge, 2 * edge)
        last = slice(2 * edge, 2 * edge + part)
        below, on = masks(edge)
        corner = low[edge : 2 * edge, edge:] + whole(second, second)
        at = put(0, low[edge : 2 * edge, :edge] + whole(second, first))
        at = put(at, jnp.where(below | on, low[:edge, :edge] + whole(first, first), corner))
        at = put(at, low[2 * edge :, :edge] + whole(last, first))
        at = put(at, jnp.broadcast_to(jnp.sum(jnp.where(on, corner, 0.0), axis=0, keepdims=True), (8, edge)))

    @pl.when(core == 1)
    def _():
        rows = step_ref[2 * edge :, :]
        both = dot_nt(jnp.concatenate([dot_nn(rows, covar), mean], axis=0), step_ref[...])
        last, low = slice(2 * edge, states), both[:edge]
        row = both[edge : edge + 1]
        if callable(added):
            low = low + added(last, slice(0, states))
            row = row + added(None, slice(0, states))
        corner = low[:, 2 * edge :]
        at = put(0, low[part:, :edge])
        at = put(at, low[:, edge : 2 * edge])
        at = put(at, corner[half:])
        at = put(at, jnp.concatenate([corner[: half // 2, :half], corner[half // 2 : half, :half]], axis=1))
        rows = [row[:, j * edge : (j + 1) * edge] for j in range(3)]
        put(at, jnp.concatenate(rows + [jnp.zeros((5, edge), F32)], axis=0))


def unpacked(mine_ref, mate_ref, covar_ref):
    states = covar_ref.shape[0]
    edge = states // 3
    half, part = edge // 2, edge * 3 // 8
    is_low = lax.rem(lax.axis_index("col"), 2) == 0
    low = jnp.where(is_low, mine_ref[...], mate_ref[...])
    high = jnp.where(is_low, mate_ref[...], mine_ref[...])
    below, on = masks(edge)

    def put(i, j, block):
        covar_ref[i * edge : (i + 1) * edge, j * edge : (j + 1) * edge] = block
        if i != j:
            covar_ref[j * edge : (j + 1) * edge, i * edge : (i + 1) * edge] = block.T

    put(1, 0, low[:edge])
    mixed = low[edge : 2 * edge]
    turned = mixed.T
    put(0, 0, jnp.where(below | on, mixed, turned))
    diagonal = low[2 * edge + part : 2 * edge + part + 1]
    put(1, 1, jnp.where(on, diagonal, jnp.where(below, turned, mixed)))
    at = edge - part
    put(2, 0, jnp.concatenate([low[2 * edge : 2 * edge + part], high[:at]], axis=0))
    put(2, 1, high[at : at + edge])
    at += edge
    bottom = high[at : at + half]
    at += half
    folded = high[at : at + half // 2]
    at += half // 2
    quarter = jnp.concatenate([folded[:, :half], folded[:, half:]], axis=0)
    top = jnp.concatenate([quarter, bottom[:, :half].T], axis=1)
    put(2, 2, jnp.concatenate([top, bottom], axis=0))
    row = jnp.concatenate([high[at + j : at + j + 1] for j in range(3)], axis=1)
    return mean_block(row, states)


def pair_covariance(
    offsets, vec_ref, corr_ref, mine_ref, mate_ref, prior_ref, start_ref, psi_ref, covar_ref, mean_ref,
    noise_other_ref, offset_other_ref, matrix_other_ref, covar_other_ref, mean_other_ref, out_ref, step_ref, work_ref,
):
    steps, states = matrix_other_ref.shape[:2]
    seg = lax.axis_index("seg")
    is_second = lax.rem(seg, 2) == 1
    last = steps - 1
    matrices_of(offsets, vec_ref, corr_ref[...], mine_ref, mate_ref, work_ref, matrix_other_ref)

    @pl.when(is_second)
    def _():
        covar_other_ref[...] = noise_other_ref[0]
        mean_other_ref[...] = offset_other_ref[0]
        step_ref[...] = psi_ref[last]

    @pl.when(seg == 1)
    def _():
        add_prior(matrix_other_ref, prior_ref, start_ref, covar_other_ref, mean_other_ref)

    @pl.when(jnp.logical_not(is_second))
    def _():
        covar_other_ref[...] = covar_ref[last]
        mean_other_ref[...] = mean_ref[last]
        step_ref[...] = matrix_other_ref[last]

    for k in range(last):
        at = k + is_second.astype(jnp.int32)
        covar, mean = square(matrix_other_ref[at], covar_other_ref[...], mean_other_ref[...])
        covar_other_ref[...] = covar + noise_other_ref[at]
        mean_other_ref[...] = mean + offset_other_ref[at]

    def added(rows, cols):
        if rows is None:
            return jnp.where(is_second, mean_ref[last, :1, cols], offset_other_ref[last, :1, cols])
        return jnp.where(is_second, covar_ref[last, rows, cols], noise_other_ref[last, rows, cols])

    put_packed(step_ref, covar_other_ref[...], mean_other_ref[...], added, out_ref)


def pair_matrices(matrix_ref, psi_ref, psi_other_ref, psi_all_ref, half_ref):
    steps, states = matrix_ref.shape[:2]
    half = states // 2
    seg = lax.axis_index("seg")
    mine = pl.ds(pl.multiple_of(lax.rem(lax.axis_index("col"), 2) * half, 8), half)

    @pl.when(seg < 2)
    def _():
        psi_other_ref[...] = jnp.zeros_like(psi_other_ref)
        psi_all_ref[...] = jnp.zeros_like(psi_all_ref)
        half_ref[...] = jnp.zeros_like(half_ref)

    @pl.when(seg >= 2)
    def _():
        psi_other_ref[...] = matrix_ref[0]
        for k in range(1, steps):
            psi_other_ref[...] = dot_nn(matrix_ref[k], psi_other_ref[...])
        own, other = psi_ref[steps - 1], psi_other_ref[...]
        is_second = lax.rem(seg, 2) == 1
        psi_all_ref[...] = dot_nn(jnp.where(is_second, own, other), jnp.where(is_second, other, own))
        half_ref[...] = psi_all_ref[mine, :]


def pair_elements(steps, width, psi_ref, covar_ref, mean_ref, psi_other_ref, psi_all_ref, covar_other_ref, mean_other_ref, *refs):
    psi_out_ref, covar_out_ref, mean_out_ref = refs
    seg = lax.axis_index("seg")
    is_second = lax.rem(seg, 2) == 1
    mine = pl.ds(pl.multiple_of(lax.axis_index("col") * width, 8), width)

    @pl.when(seg < 2)
    def _():
        psi_out_ref[...] = jnp.zeros_like(psi_out_ref)

    @pl.when((seg >= 2) & is_second)
    def _():
        for k in range(steps - 1):
            psi_out_ref[k] = dot_nn(psi_ref[k], psi_other_ref[...])
        psi_out_ref[steps - 1] = psi_all_ref[...]

    @pl.when((seg >= 2) & jnp.logical_not(is_second))
    def _():
        psi_out_ref[...] = psi_ref[...]

    @pl.when(is_second)
    def _():
        covar, mean = covar_other_ref[...], mean_other_ref[...]
        for k in range(steps):
            half = dot_nn(psi_ref[k, mine, :], covar)
            both = dot_nt(jnp.concatenate([half, mean], axis=0), psi_ref[k])
            covar_out_ref[k] = both[:width] + covar_ref[k, mine, :]
            mean_out_ref[k] = both[width:] + mean_ref[k]

    @pl.when(jnp.logical_not(is_second))
    def _():
        for k in range(steps):
            covar_out_ref[k] = covar_ref[k, mine, :]
            mean_out_ref[k] = mean_ref[k]


def whole_matrix(mine, mate):
    is_low = lax.rem(lax.axis_index("col"), 2) == 0
    return jnp.concatenate([jnp.where(is_low, mine, mate), jnp.where(is_low, mate, mine)], axis=0)


def place_in(bit):
    return lax.div(lax.rem(lax.axis_index("seg"), 2 * bit) - bit, 2) - (lax.rem(lax.axis_index("seg"), 2 * bit) < bit)


def is_upper(bit):
    return lax.rem(lax.axis_index("seg"), 2 * bit) >= bit


def chosen(refs, bit):
    at = place_in(bit)
    value = refs[0][...]
    for i, ref in enumerate(refs[1:]):
        value = jnp.where(at == i + 1, ref[...], value)
    return value


def joined_covariance(bit, psi_ref, total_ref, *refs):
    n_group = bit // 2
    mines, mates = refs[:n_group], refs[n_group : 2 * n_group]
    out_ref, mine_ref, mate_ref, work_ref = refs[2 * n_group :]

    seg, last = lax.axis_index("seg"), lax.axis_size("seg") - 2

    @pl.when((lax.rem(seg, 2 * bit) >= 2 * bit - 2) & (seg < last))
    def _():
        mine_ref[...] = chosen(mines, bit)
        mate_ref[...] = chosen(mates, bit)
        mean = unpacked(mine_ref, mate_ref, work_ref)
        put_packed(psi_ref, work_ref[...], mean, total_ref, out_ref)


def chosen_matrix(refs, bit):
    n_group = bit // 2
    mine, *mate = [chosen(refs[i * n_group : (i + 1) * n_group], bit) for i in range(3)]
    return whole_matrix(mine, jnp.concatenate(mate, axis=0))


def joined_matrix(bit, psi_ref, *refs):
    refs[-1][...] = dot_nn(psi_ref[...], chosen_matrix(refs[:-1], bit))


def entered(bit, psi_ref, covar_ref, mean_ref, *refs):
    n_group = bit // 2
    mines, mates = refs[:n_group], refs[n_group : 2 * n_group]
    covar_out_ref, mean_out_ref, mine_ref, mate_ref, work_ref = refs[2 * n_group :]
    steps, width, states = covar_ref.shape
    mine = pl.ds(pl.multiple_of(lax.axis_index("col") * width, 8), width)

    @pl.when(is_upper(bit))
    def _():
        mine_ref[...] = chosen(mines, bit)
        mate_ref[...] = chosen(mates, bit)
        mean = unpacked(mine_ref, mate_ref, work_ref)
        covar = work_ref[...]
        for k in range(steps):
            half = dot_nn(psi_ref[k, mine, :], covar)
            both = dot_nt(jnp.concatenate([half, mean], axis=0), psi_ref[k])
            covar_out_ref[k] = both[:width] + covar_ref[k]
            mean_out_ref[k] = both[width:] + mean_ref[k]

    @pl.when(jnp.logical_not(is_upper(bit)))
    def _():
        covar_out_ref[...] = covar_ref[...]
        mean_out_ref[...] = mean_ref[...]


def takes_matrix(bit):
    return is_upper(bit) & (lax.axis_index("seg") >= 2 * bit)


def matrices_entered(bit, psi_ref, *refs):
    psi_out_ref = refs[-1]

    @pl.when(takes_matrix(bit))
    def _():
        before = chosen_matrix(refs[:-1], bit)
        for k in range(psi_ref.shape[0]):
            psi_out_ref[k] = dot_nn(psi_ref[k], before)

    @pl.when(jnp.logical_not(takes_matrix(bit)))
    def _():
        psi_out_ref[...] = psi_ref[...]


def finished(bit, psi_ref, covar_ref, mean_ref, *refs):
    n_group = bit // 2
    mines, mates = refs[:n_group], refs[n_group : 2 * n_group]
    covar_out_ref, mean_out_ref, mine_ref, mate_ref, work_ref = refs[2 * n_group :]
    steps, width, states = covar_ref.shape
    mine = pl.ds(pl.multiple_of(lax.axis_index("col") * width, 8), width)

    @pl.when(is_upper(bit))
    def _():
        mine_ref[...] = chosen(mines, bit)
        mate_ref[...] = chosen(mates, bit)
        mean = unpacked(mine_ref, mate_ref, work_ref)
        rows = jnp.concatenate([psi_ref[k, mine, :] for k in range(steps)], axis=0)
        half = few_rows_dot(rows, work_ref[...], NN)
        for k in range(steps):
            part = half[k * width : (k + 1) * width]
            both = few_rows_dot(jnp.concatenate([part, mean], axis=0), psi_ref[k], NT)
            covar_out_ref[k] = both[:width] + covar_ref[k]
            mean_out_ref[k : k + 1, :] = both[width : width + 1] + mean_ref[k, :1, :]

    @pl.when(jnp.logical_not(is_upper(bit)))
    def _():
        covar_out_ref[...] = covar_ref[...]
        for k in range(steps):
            mean_out_ref[k : k + 1, :] = mean_ref[k, :1, :]


def swapped(block, axis, bit):
    return lax.ppermute(block, axis, [(i, i ^ bit) for i in range(lax.axis_size(axis))])


def handed_up(block, bit, first=0):
    n_seg, n_col = lax.axis_size("seg"), lax.axis_size("col")
    came = []
    for group in reversed(range(bit // 2)):
        aside = n_col // 2 if group % 2 == 0 else n_col
        to = {i: i ^ aside for i in range(n_seg * n_col)}
        for low in range(first * 2 * bit, n_seg, 2 * bit):
            for i in range((low + bit - 2) * n_col, (low + bit) * n_col):
                j = i + (2 + 2 * group) * n_col
                to[i], to[j] = j, i
        came.insert(0, lax.ppermute(block, ("seg", "col"), sorted(to.items())))
    return came


def with_mate(share):
    return (share, swapped(share, "col", 1))


def per_device(
    model_mixing,
    retention,
    forcing,
    observations,
    model_noise,
    obs_noise,
    gain,
    obs_operator_t,
    prior_mean,
    prior_factor,
):
    steps, width, states = model_mixing.shape
    n_col, n_seg = lax.axis_size("col"), lax.axis_size("seg")
    col = lax.axis_index("col")
    edge = states // 3
    square_shape, mean_shape = (states, states), (MEAN_ROWS, states)
    share_shape, half_shape = (share_rows(edge), edge), (states // 2, states)
    far_bits = []
    bit = n_col // 2
    while bit > 1:
        far_bits.append(bit)
        bit //= 2
    offsets = [0]
    for bit in far_bits:
        offsets = offsets + [o ^ bit for o in offsets]

    own = [model_mixing]
    for bit in far_bits:
        own = own + [swapped(b, "col", bit) for b in own]
    near = swapped(model_mixing, "seg", 1)
    corr_mine, vectors = local_call(
        correction_rows,
        [(width, states), (steps, 4, states)],
        gain,
        obs_operator_t,
        observations,
        retention,
        forcing,
        model_noise,
        copied=True,
        cost=3,
    )
    corr_mine, gain = lax.optimization_barrier((corr_mine, gain))
    fixed, prior = local_call(
        fixed_parts, [square_shape, square_shape], gain, obs_noise[None, :], prior_factor
    )
    corr = [corr_mine]
    for bit in far_bits:
        corr = corr + [swapped(b, "col", bit) for b in corr]
    vectors_other = swapped(vectors, "seg", 1)
    own, near, fixed, vectors_other = lax.optimization_barrier((own, near, fixed, vectors_other))
    other = [near] + [swapped(b, "seg", 1) for b in own[1:]]
    corr = corr + [swapped(b, "col", 1) for b in corr]
    rows_shape = (steps,) + half_shape
    noise_shapes = [(steps,) + square_shape, (steps,) + mean_shape]
    correction, rows, push, push_other = local_call(
        functools.partial(own_rows, offsets + [o ^ 1 for o in offsets]),
        [square_shape, rows_shape, (steps, states), (steps, states)],
        vectors,
        vectors_other,
        *corr,
        *own,
        scratch=[square_shape],
    )
    noise, offset = local_call(noises, noise_shapes, vectors, push, fixed, correction)
    start = prior_mean[None, :]
    noise_other, offset_other = local_call(
        noises, noise_shapes, vectors_other, push_other, fixed, correction
    )
    other, correction, noise, noise_other = lax.optimization_barrier((other, correction, noise, noise_other))
    (rows_other,) = local_call(other_rows, [rows_shape], correction, *other)
    matrix, psi, covar, mean = local_call(
        functools.partial(own_segment, offsets),
        [(steps,) + square_shape, (steps,) + square_shape, (steps,) + square_shape, (steps,) + mean_shape],
        vectors,
        correction,
        *with_mate(rows),
        noise,
        offset,
        prior,
        start,
        scratch=[square_shape],
        cost=1,
    )
    bit = 2
    more = 2 * bit < n_seg
    matrix_other, covar_other, mean_other, total = local_call(
        functools.partial(pair_covariance, offsets),
        [(steps,) + square_shape, square_shape, mean_shape, share_shape],
        vectors_other,
        correction,
        *with_mate(rows_other),
        prior,
        start,
        psi,
        covar,
        mean,
        noise_other,
        offset_other,
        scratch=[square_shape, square_shape],
    )
    came = handed_up(total, bit)
    matrix_other, total = lax.optimization_barrier((matrix_other, total))
    psi_other, psi_all, psi_half = local_call(
        pair_matrices, [square_shape, square_shape, half_shape], matrix_other, psi
    )
    step = []
    if more:
        step = handed_up(psi_half, bit, 1)
    psi, covar, mean = local_call(
        functools.partial(pair_elements, steps, width),
        [(steps,) + square_shape, (steps, width, states), (steps,) + mean_shape],
        psi,
        covar,
        mean,
        psi_other,
        psi_all,
        covar_other,
        mean_other,
    )

    def over_core(blocks):
        return list(blocks) + [swapped(b, "col", 1) for b in blocks]

    while more:
        more = 4 * bit < n_seg
        came, psi_all, psi = lax.optimization_barrier((came, psi_all, psi))
        came = over_core(came)
        (total,) = local_call(
            functools.partial(joined_covariance, bit),
            [share_shape],
            psi_all,
            total,
            *came,
            scratch=[share_shape, share_shape, square_shape],
        )
        came_next = handed_up(total, 2 * bit)
        covar, total = lax.optimization_barrier((covar, total))
        covar, mean = local_call(
            functools.partial(entered, bit),
            [(steps, width, states), (steps,) + mean_shape],
            psi,
            covar,
            mean,
            *came,
            scratch=[share_shape, share_shape, square_shape],
        )
        step, covar = lax.optimization_barrier((step, covar))
        for part in (slice(0, states // 4), slice(states // 4, states // 2)):
            step = step + [swapped(b[part], "col", 1) for b in step[: bit // 2]]
        if more:
            (psi_all,) = local_call(functools.partial(joined_matrix, bit), [square_shape], psi_all, *step)
            psi_half = lax.dynamic_slice_in_dim(psi_all, col % 2 * (states // 2), states // 2, 0)
        (psi,) = local_call(
            functools.partial(matrices_entered, bit), [(steps,) + square_shape], psi, *step
        )
        if more:
            step = handed_up(psi_half, 2 * bit, 1)
        came = came_next
        bit *= 2
    came, covar, psi = lax.optimization_barrier((came, covar, psi))
    covars, means = local_call(
        functools.partial(finished, bit),
        [(steps, width, states), (steps, states)],
        psi,
        covar,
        mean,
        *over_core(came),
        scratch=[share_shape, share_shape, square_shape],
    )
    return means, covars


def solution(mesh):
    in_specs = (
        P("seg", "col", None),
        P("seg", None),
        P("seg", None),
        P("seg", None),
        P("seg", None),
        P(),
        P(),
        P("col", None),
        P(),
        P(),
    )
    out_specs = (P("seg", None), P("seg", "col", None))
    return jax.shard_map(
        per_device, mesh=mesh, in_specs=in_specs, out_specs=out_specs, check_vma=False
    )
```
